128 devices in a mesh: row: 32 (over z, x, y_lo), ch: 4 (over y_hi, core).
Axes of the slice: x: 4, y: 4 (y_hi: 2, y_lo: 2; y = y_hi * 2 + y_lo), z: 4, core: 2. Of those that a mesh axis runs over, the one named last changes fastest.
Arguments:
- pair_in: bfloat16 [512, 512, 128], P('row', 'ch'), may hold values from -6 to 6
- grad_out: bfloat16 [512, 512, 128], P('row', 'ch'), may hold values from -6 to 6
- token_valid: int32 [512], replicated, may hold values from 0 to 1, as said below
- chain_ids: int32 [512], replicated, may hold values from 0 to 7, never falling along the last dimension, each value on 1 to 128 neighbouring positions
- chain_table: float32 [2, 128], replicated, may hold values from -4 to 4
- norm_gain: float32 [2, 2, 128], replicated, may hold values from 0.1 to 1.9
- norm_offset: float32 [2, 2, 128], replicated, may hold values from -3 to 3
- proj_in: bfloat16 [2, 128, 640], replicated, may hold values from -0.5 to 0.5
- proj_out: bfloat16 [2, 128, 128], replicated, may hold values from -0.5 to 0.5
Outputs:
- final_pair: bfloat16 [512, 512, 128], P('row', 'ch')
- pair_grad: bfloat16 [512, 512, 128], P('row', 'ch')
The draws below stay inside these ranges and needn't reach their ends.
Inputs may be any that keep to these rules, and one draw needn't show every extreme that they name: token_valid is 1 on a leading run of at least 256 tokens and 0 on the rest; the last token is always padding. `chain_ids`: chain ids never fall along the crop.
All inputs are finite; a program needn't handle non-finite values.
Results may differ from the reference program's by a relative error of at most 0.0075.
Values may be sent and summed in bfloat16 or wider, within the bound.
A program may use at most 128 MiB of HBM per device.

```python
import math
import jax
import jax.numpy as jnp
import numpy as np
from jax import lax

PAIR = 128
TOKENS = 512


def draw_token_valid(key, part):
    key = jax.random.fold_in(key, 11)
    length = jax.random.randint(key, (), TOKENS // 2, TOKENS)
    return (jnp.arange(TOKENS) < length).astype(jnp.int32)


def steps_of(rng, shape, pieces, smallest, top_value):
    def one(axis_at, blocks):
        heights = jax.random.uniform(jax.random.fold_in(jax.random.fold_in(rng, 6), axis_at), (blocks,), jnp.float32, smallest / len(pieces), top_value / len(pieces))
        return jnp.repeat(jnp.exp(heights), shape[axis_at] // blocks).reshape((-1,) + (1,) * (len(shape) - axis_at - 1))

    gain = one(*pieces[0])
    for cut in pieces[1:]:
        gain = gain * one(*cut)
    return gain


def length_profile(amount, total, bound, skew):
    portions = [(1 << 20) // math.isqrt(rank ** skew) + 1 for rank in range(2, amount + 1)]
    spare, counts = total - bound - (amount - 1), [1] * (amount - 1)
    while spare > 0:
        movable = [i for i in range(amount - 1) if counts[i] < bound]
        pool, budget = sum([portions[i] for i in movable]), spare
        for i in movable:
            addition = min(bound - counts[i], max(1, budget * portions[i] // pool), spare)
            counts[i] = counts[i] + addition
            spare = spare - addition
    return np.array([bound] + counts)


def uneven_parts(stream_key, amount, total, limit, slope):
    if amount == 2:
        one = jax.random.randint(stream_key, (), max(1, total - limit), min(limit, total - 1) + 1)
        return jnp.stack([one, total - one])
    lengths = jnp.asarray(length_profile(amount, total, limit, slope), jnp.int32)
    pairs = (amount - 1) // 2
    giver, sink = lengths[1:1 + 2 * pairs:2], lengths[2:2 + 2 * pairs:2]
    slack = jnp.minimum(giver - 1, limit - sink)
    moved = jax.random.randint(jax.random.fold_in(stream_key, 1), (pairs,), 0, 1 << 20) % (slack + 1)
    lengths = lengths.at[1:1 + 2 * pairs:2].set(giver - moved).at[2:2 + 2 * pairs:2].set(sink + moved)
    return lengths[jax.random.permutation(jax.random.fold_in(stream_key, 2), amount)]


def scatter_about(rng, shape, scale, limit, shards=(), dtype=jnp.bfloat16):
    factor_of = steps_of(rng, shape, shards, -0.22, 0.18) if shards else 1.0
    array = jax.random.normal(rng, shape, jnp.float32) * scale * factor_of
    return jnp.minimum(jnp.maximum(array, -limit), limit).astype(dtype)


def setup_inputs(seed: int = 0) -> dict:
    keys = jax.random.split(jax.random.key(seed), 10)
    return {
        "pair_in": scatter_about(keys[0], (TOKENS, TOKENS, PAIR), 1.0, 6.0, ((0, 32), (1, 4))),
        "grad_out": scatter_about(keys[1], (TOKENS, TOKENS, PAIR), 1.0, 6.0, ((0, 32), (1, 4))),
        "token_valid": draw_token_valid(jax.random.fold_in(keys[9], 71), 0),
        "chain_ids": jnp.searchsorted(jnp.cumsum(uneven_parts(keys[3], 8, TOKENS, TOKENS // 4, 1)), jnp.arange(TOKENS), side="right").astype(jnp.int32),
        "chain_table": scatter_about(keys[4], (2, PAIR), 1.0, 4.0, (), jnp.float32),
        "norm_gain": jnp.clip(1.0 + 0.18 * jax.random.normal(keys[5], (2, 2, PAIR), jnp.float32), 0.1, 1.9),
        "norm_offset": scatter_about(keys[6], (2, 2, PAIR), 0.5, 3.0, (), jnp.float32),
        "proj_in": scatter_about(keys[7], (2, PAIR, 5 * PAIR), PAIR ** -0.5, 0.5),
        "proj_out": scatter_about(keys[8], (2, PAIR, PAIR), PAIR ** -0.5, 0.5),
    }


EPS = 1e-05

def layer_norm(values, norm_scale, norm_shift):
    average = lax.optimization_barrier(jnp.mean(values, axis=-1, keepdims=True))
    centred = values - average
    spread = lax.optimization_barrier(jnp.mean(centred * centred, axis=-1, keepdims=True))
    return centred * lax.rsqrt(spread + EPS) * norm_scale + norm_shift

def gated(linear):
    gate_part, value_part = jnp.split(linear, 2, axis=-1)
    return jax.nn.sigmoid(gate_part) * value_part

def gated_back(linear, upstream):
    gate_part, value_part = jnp.split(linear, 2, axis=-1)
    squash = jax.nn.sigmoid(gate_part)
    return jnp.concatenate([upstream * value_part * squash * (1.0 - squash), upstream * squash], axis=-1)

def forward_block(block_in, pair_mask, gains, offsets, weight_in, weight_out, outgoing):
    pair_width = weight_in.shape[0]
    input32 = block_in.astype(jnp.float32)
    normed = layer_norm(input32, gains[0], offsets[0]).astype(jnp.bfloat16)
    lin_left = jnp.dot(normed, weight_in[:, :2 * pair_width], preferred_element_type=jnp.float32)
    lin_right = jnp.dot(normed, weight_in[:, 2 * pair_width:4 * pair_width], preferred_element_type=jnp.float32)
    lin_gate = jnp.dot(normed, weight_in[:, 4 * pair_width:], preferred_element_type=jnp.float32)
    left_factor = (pair_mask[:, :, None] * gated(lin_left)).astype(jnp.bfloat16)
    right_factor = (pair_mask[:, :, None] * gated(lin_right)).astype(jnp.bfloat16)
    gate_value = jax.nn.sigmoid(lin_gate)
    if outgoing:
        triangle = jnp.einsum('ikc,jkc->ijc', left_factor.astype(jnp.float32), right_factor.astype(jnp.float32))
    else:
        triangle = jnp.einsum('kic,kjc->ijc', left_factor.astype(jnp.float32), right_factor.astype(jnp.float32))
    triangle = triangle.astype(jnp.bfloat16)
    tri_norm = layer_norm(triangle.astype(jnp.float32), gains[1], offsets[1]).astype(jnp.bfloat16)
    mixed_out = jnp.dot(tri_norm, weight_out, preferred_element_type=jnp.float32)
    block_out = (input32 + gate_value * mixed_out).astype(jnp.bfloat16)
    return (block_out, (input32, lin_left, lin_right, gate_value, left_factor, right_factor, triangle, mixed_out))

def backward_block(grad_in, saved, pair_mask, gains, offsets, weight_in, weight_out, outgoing):
    input32, lin_left, lin_right, gate_value, left_factor, right_factor, triangle, mixed_out = saved
    pair_width = weight_in.shape[0]
    upstream = grad_in.astype(jnp.float32)
    grad_gate = upstream * mixed_out
    grad_mixed = (upstream * gate_value).astype(jnp.bfloat16)
    grad_tnorm = jnp.dot(grad_mixed, weight_out.T, preferred_element_type=jnp.float32)
    _, out_back = jax.vjp(lambda values: layer_norm(values, gains[1], offsets[1]), triangle.astype(jnp.float32))
    grad_tri = out_back(grad_tnorm)[0].astype(jnp.bfloat16).astype(jnp.float32)
    left32 = left_factor.astype(jnp.float32)
    right32 = right_factor.astype(jnp.float32)
    if outgoing:
        grad_left = jnp.einsum('ijc,jkc->ikc', grad_tri, right32)
        grad_right = jnp.einsum('ijc,ikc->jkc', grad_tri, left32)
    else:
        grad_left = jnp.einsum('ijc,kjc->kic', grad_tri, right32)
        grad_right = jnp.einsum('ijc,kic->kjc', grad_tri, left32)
    grad_left = grad_left.astype(jnp.bfloat16).astype(jnp.float32)
    grad_right = grad_right.astype(jnp.bfloat16).astype(jnp.float32)
    grad_lin_left = gated_back(lin_left, pair_mask[:, :, None] * grad_left).astype(jnp.bfloat16)
    grad_lin_right = gated_back(lin_right, pair_mask[:, :, None] * grad_right).astype(jnp.bfloat16)
    grad_lin_gate = (grad_gate * gate_value * (1.0 - gate_value)).astype(jnp.bfloat16)
    grad_normed = jnp.dot(grad_lin_left, weight_in[:, :2 * pair_width].T, preferred_element_type=jnp.float32) + jnp.dot(grad_lin_right, weight_in[:, 2 * pair_width:4 * pair_width].T, preferred_element_type=jnp.float32) + jnp.dot(grad_lin_gate, weight_in[:, 4 * pair_width:].T, preferred_element_type=jnp.float32)
    _, in_back = jax.vjp(lambda values: layer_norm(values, gains[0], offsets[0]), input32)
    return (upstream + in_back(grad_normed)[0]).astype(jnp.bfloat16)

def reference(pair_in, grad_out, token_valid, chain_ids, chain_table, norm_gain, norm_offset, proj_in, proj_out):
    valid32 = token_valid.astype(jnp.float32)
    pair_mask = valid32[:, None] * valid32[None, :]
    same_chain = (chain_ids[:, None] == chain_ids[None, :]).astype(jnp.float32)[:, :, None]
    entry_pair = (pair_in.astype(jnp.float32) + same_chain * chain_table[1] + (1.0 - same_chain) * chain_table[0]).astype(jnp.bfloat16)
    middle, first_saved = forward_block(entry_pair, pair_mask, norm_gain[0], norm_offset[0], proj_in[0], proj_out[0], True)
    final_pair, second_saved = forward_block(middle, pair_mask, norm_gain[1], norm_offset[1], proj_in[1], proj_out[1], False)
    grad_middle = backward_block(grad_out, second_saved, pair_mask, norm_gain[1], norm_offset[1], proj_in[1], proj_out[1], False)
    pair_grad = backward_block(grad_middle, first_saved, pair_mask, norm_gain[0], norm_offset[0], proj_in[0], proj_out[0], True)
    return (final_pair, pair_grad)
```

```python
import jax
import jax.numpy as jnp
from jax import lax
from jax.sharding import PartitionSpec as P
from jax.experimental import pallas as pl
from jax.experimental.pallas import tpu as pltpu

EPS = 1e-05
MESH = pl.DeviceIdType.MESH
DEVICES = 128
UNITS = 12
SLABS = 8


def far_first(digit):
    return (digit + 2) - lax.div(digit, 2) * (2 * digit - 1)


def dot(first, second, first_dim=1, second_dim=0):
    return lax.dot_general(
        first,
        second,
        (((first_dim,), (second_dim,)), ((), ())),
        preferred_element_type=jnp.float32,
    )


def normalise(values):
    average = jnp.mean(values, axis=0, keepdims=True)
    centred = values - average
    spread = jnp.mean(centred * centred, axis=0, keepdims=True)
    inverse = lax.rsqrt(spread + EPS)
    return centred * inverse, inverse


def normalise_back(scaled_grad, unit, inverse):
    mean_grad = jnp.mean(scaled_grad, axis=0, keepdims=True)
    mean_prod = jnp.mean(scaled_grad * unit, axis=0, keepdims=True)
    return inverse * (scaled_grad - mean_grad - unit * mean_prod)


def twice(block):
    return jnp.concatenate([block, block], axis=1)


def kernel(
    pair_ref,
    gout_ref,
    valid_s,
    chain_s,
    valid_v,
    chain_v,
    table_ref,
    gain_ref,
    offset_ref,
    win_ref,
    wout_ref,
    final_ref,
    grad_ref,
    par,
    win_t,
    wout_t,
    mask,
    held,
    normed,
    lin,
    unit_t,
    inv_t,
    mixed_s,
    gtn,
    tnorm,
    gnorm,
    upper,
    stage_a,
    stage_b,
    snd,
    rcv,
    ssem,
    rsem,
):
    row, col = lax.axis_index("row"), lax.axis_index("ch")
    z, x = lax.div(row, 8), lax.rem(lax.div(row, 2), 4)
    y, core = lax.div(col, 2) * 2 + lax.rem(row, 2), lax.rem(col, 2)
    me = col * 32 + row

    def partner(t):
        z2 = lax.rem(z + far_first(lax.rem(lax.div(t, 16), 4)), 4)
        x2 = lax.rem(x + far_first(lax.rem(lax.div(t, 4), 4)), 4)
        y2 = lax.rem(y + far_first(lax.rem(t, 4)), 4)
        c2 = lax.rem(core + 1 - lax.div(t, 64), 2)
        return z2 * 8 + x2 * 2 + lax.rem(y2, 2), lax.div(y2, 2) * 2 + c2

    barrier = pltpu.get_barrier_semaphore()

    def greet(t, carry):
        pl.semaphore_signal(barrier, inc=1, device_id=partner(t), device_id_type=MESH)
        return carry

    lax.fori_loop(0, DEVICES - 1, greet, 0)

    def send(u):
        rcv[u, me] = snd[u, me]

        def step(t, carry):
            r2, h2 = partner(t)
            pltpu.make_async_remote_copy(
                src_ref=snd.at[u, h2 * 32 + r2],
                dst_ref=rcv.at[u, me],
                send_sem=ssem.at[u],
                recv_sem=rsem.at[u],
                device_id=(r2, h2),
                device_id_type=MESH,
            ).start()
            return carry

        lax.fori_loop(0, DEVICES - 1, step, 0)

    def whole(u):
        return pltpu.make_async_remote_copy(
            src_ref=snd.at[u, pl.ds(0, DEVICES - 1)],
            dst_ref=rcv.at[u, pl.ds(0, DEVICES - 1)],
            send_sem=ssem.at[u],
            recv_sem=rsem.at[u],
            device_id=(row, col),
            device_id_type=MESH,
        )

    def each_slab(body):
        def step(s, carry):
            body(s)
            return carry

        lax.fori_loop(0, SLABS, step, 0)

    def put(stage, s, value):
        stage[pl.ds(2 * s, 128, stride=16), :] = value[:, :128]
        stage[pl.ds(2 * s + 1, 128, stride=16), :] = value[:, 128:]

    def get(stage, s):
        return jnp.concatenate(
            [stage[pl.ds(2 * s, 128, stride=16), :], stage[pl.ds(2 * s + 1, 128, stride=16), :]],
            axis=1,
        )

    def flush(stage, u):
        def step(q, carry):
            part = stage[pl.ds(pl.multiple_of(q * 256, 256), 256), :]
            snd[u, pl.ds(q * 16, 16)] = part.astype(jnp.bfloat16).reshape(16, 16, 128)
            return carry

        lax.fori_loop(0, 8, step, 0)
        send(u)

    def fetch(u, stage):
        whole(u).wait_recv()

        def step(q, carry):
            part = rcv[u, pl.ds(q * 16, 16)].reshape(256, 128)
            stage[pl.ds(pl.multiple_of(q * 256, 256), 256), :] = part.astype(jnp.float32)
            return carry

        lax.fori_loop(0, 8, step, 0)

    def gain(layer, which):
        return twice(par[2 + 2 * layer + which])

    def offset(layer, which):
        return twice(par[6 + 2 * layer + which])

    def column(row_values):
        return jnp.transpose(jnp.broadcast_to(row_values, (128, 128)))

    def prepare(layer):
        for which in range(2):
            k = 2 * layer + which
            par[2 + k] = column(gain_ref[k : k + 1, :])
            par[6 + k] = column(offset_ref[k : k + 1, :])
        for part in range(5):
            block = win_ref[layer, :, part * 128 : (part + 1) * 128].astype(jnp.float32)
            win_t[layer, part * 128 : (part + 1) * 128, :] = jnp.transpose(block).astype(
                jnp.bfloat16
            )
        wout_t[layer] = jnp.transpose(wout_ref[layer].astype(jnp.float32)).astype(jnp.bfloat16)

    def matrix(u, first=0, count=32):
        return jnp.concatenate(
            [
                rcv[u, 32 * h + first : 32 * h + first + count].reshape(16 * count, 128)
                for h in range(4)
            ],
            axis=1,
        )

    def multiply(u_first, flip_first, u_second, flip_second, u_out):
        second = matrix(u_second)
        for m in range(2):
            if flip_first:
                first = jnp.concatenate(
                    [
                        rcv[u_first, 32 * h : 32 * h + 32].reshape(512, 128)
                        for h in (2 * m, 2 * m + 1)
                    ],
                    axis=1,
                )
            else:
                first = matrix(u_first, 16 * m, 16)
            result = dot(first, second, 0 if flip_first else 1, 1 if flip_second else 0)
            result = result.astype(jnp.bfloat16)
            for h in range(4):
                snd[u_out, 32 * h + 16 * m : 32 * h + 16 * m + 16] = result[
                    :, 128 * h : 128 * h + 128
                ].reshape(16, 16, 128)
        send(u_out)

    def factor(layer, s, part, stage):
        both = dot(win_t[layer, 256 * part : 256 * part + 256, :], normed[s])
        squash = jax.nn.sigmoid(both[:128])
        value = both[128:]
        lin[layer, s, 256 * part : 256 * part + 128, :] = squash
        lin[layer, s, 256 * part + 128 : 256 * part + 256, :] = value
        put(stage, s, mask[s, 0:1, :] * (squash * value))

    def input_norm(layer, s, values):
        unit, _ = normalise(values)
        normed[s] = (unit * gain(layer, 0) + offset(layer, 0)).astype(jnp.bfloat16)

    def open_gate(layer, s):
        lin[layer, s, 512:640, :] = jax.nn.sigmoid(dot(win_t[layer, 512:640, :], normed[s]))

    def product_norm(layer, s, stage):
        unit, inverse = normalise(get(stage, s))
        return unit, inverse, (unit * gain(layer, 1) + offset(layer, 1)).astype(jnp.bfloat16)

    def mixed_back(layer, s, upstream):
        grad_mixed = (upstream * lin[layer, s, 512:640, :]).astype(jnp.bfloat16)
        return dot(wout_ref[layer], grad_mixed)

    def gate_back(layer, s, upstream, mixed):
        gate = lin[layer, s, 512:640, :]
        back = (upstream * mixed * gate * (1.0 - gate)).astype(jnp.bfloat16)
        gnorm[s] = dot(win_ref[layer, :, 512:640], back)

    def factor_back(layer, s, part, stage):
        squash = lin[layer, s, 256 * part : 256 * part + 128, :]
        value = lin[layer, s, 256 * part + 128 : 256 * part + 256, :]
        cotangent = mask[s, 0:1, :] * get(stage, s)
        last = cotangent * squash
        first = last * value * (1.0 - squash)
        both = jnp.concatenate([first.astype(jnp.bfloat16), last.astype(jnp.bfloat16)], axis=0)
        return gnorm[s] + dot(win_ref[layer, :, 256 * part : 256 * part + 256], both)

    def input_back(layer, s, grad_normed):
        unit, inverse = normalise(held[layer, s].astype(jnp.float32))
        back = normalise_back(grad_normed * gain(layer, 0), unit, inverse)
        return (upper[s].astype(jnp.float32) + back).astype(jnp.bfloat16)

    par[0] = column(table_ref[0:1, :])
    par[1] = column(table_ref[1:2, :])
    prepare(0)
    valid_cols = valid_v[pl.ds(col, 1), :].astype(jnp.float32)
    chain_cols = chain_v[pl.ds(col, 1), :]

    def enter(s):
        parts, masks = [], []
        for k in range(2):
            at = row * 16 + 2 * s + k
            masks.append(valid_s[at].astype(jnp.float32) * valid_cols)
            same = (chain_cols == chain_s[at]).astype(jnp.float32)
            block = jnp.transpose(pair_ref[2 * s + k].astype(jnp.float32))
            parts.append(block + same * par[1] + (1.0 - same) * par[0])
        mask[s] = jnp.broadcast_to(jnp.concatenate(masks, axis=1), (8, 256))
        entry = jnp.concatenate(parts, axis=1).astype(jnp.bfloat16)
        held[0, s] = entry
        input_norm(0, s, entry.astype(jnp.float32))
        factor(0, s, 0, stage_a)

    each_slab(enter)
    pl.semaphore_wait(barrier, DEVICES - 1)
    flush(stage_a, 0)
    each_slab(lambda s: factor(0, s, 1, stage_b))
    flush(stage_b, 1)

    def rest_of_entry(s):
        open_gate(0, s)
        parts = [jnp.transpose(gout_ref[2 * s + k].astype(jnp.float32)) for k in range(2)]
        upper[s] = jnp.concatenate(parts, axis=1).astype(jnp.bfloat16)

    each_slab(rest_of_entry)
    prepare(1)
    whole(0).wait_recv()
    whole(1).wait_recv()
    multiply(0, False, 1, True, 2)

    fetch(2, stage_a)

    def middle(s):
        unit, inverse, scaled = product_norm(0, s, stage_a)
        unit_t[s] = unit
        inv_t[s] = jnp.broadcast_to(inverse, (8, 256))
        mixed = dot(wout_t[0], scaled)
        mixed_s[s] = mixed
        value = held[0, s].astype(jnp.float32) + lin[0, s, 512:640, :] * mixed
        value = value.astype(jnp.bfloat16)
        held[1, s] = value
        input_norm(1, s, value.astype(jnp.float32))
        factor(1, s, 0, stage_b)

    each_slab(middle)
    flush(stage_b, 3)
    each_slab(lambda s: factor(1, s, 1, stage_a))
    flush(stage_a, 4)

    def rest_of_middle(s):
        open_gate(1, s)
        gtn[s] = mixed_back(1, s, upper[s].astype(jnp.float32))

    each_slab(rest_of_middle)
    whole(3).wait_recv()
    whole(4).wait_recv()
    multiply(3, True, 4, False, 5)

    fetch(5, stage_a)

    def turn(s):
        unit, inverse, scaled = product_norm(1, s, stage_a)
        tnorm[s] = scaled
        put(stage_b, s, normalise_back(gtn[s] * gain(1, 1), unit, inverse))

    each_slab(turn)
    flush(stage_b, 6)

    def finish(s):
        mixed = dot(wout_t[1], tnorm[s])
        value = held[1, s].astype(jnp.float32) + lin[1, s, 512:640, :] * mixed
        for k in range(2):
            final_ref[2 * s + k] = jnp.transpose(value[:, 128 * k : 128 * k + 128]).astype(
                jnp.bfloat16
            )
        gate_back(1, s, upper[s].astype(jnp.float32), mixed)

    each_slab(finish)
    whole(6).wait_recv()
    multiply(4, False, 6, True, 7)
    multiply(3, False, 6, False, 8)
    fetch(7, stage_a)

    def left_back(layer, s):
        gnorm[s] = factor_back(layer, s, 0, stage_a)

    each_slab(lambda s: left_back(1, s))
    fetch(8, stage_b)

    def lower(s):
        value = input_back(1, s, factor_back(1, s, 1, stage_b))
        upper[s] = value
        grad_tnorm = mixed_back(0, s, value.astype(jnp.float32))
        put(stage_a, s, normalise_back(grad_tnorm * gain(0, 1), unit_t[s], inv_t[s, 0:1, :]))

    each_slab(lower)
    flush(stage_a, 9)
    each_slab(lambda s: gate_back(0, s, upper[s].astype(jnp.float32), mixed_s[s]))
    whole(9).wait_recv()
    multiply(9, False, 1, False, 10)
    multiply(9, True, 0, False, 11)
    fetch(10, stage_a)
    each_slab(lambda s: left_back(0, s))
    fetch(11, stage_b)

    def leave(s):
        value = input_back(0, s, factor_back(0, s, 1, stage_b)).astype(jnp.float32)
        for k in range(2):
            grad_ref[2 * s + k] = jnp.transpose(value[:, 128 * k : 128 * k + 128]).astype(
                jnp.bfloat16
            )

    each_slab(leave)
    for u in range(UNITS):
        whole(u).wait_send()


def local(
    pair_in,
    grad_out,
    token_valid,
    chain_ids,
    chain_table,
    norm_gain,
    norm_offset,
    proj_in,
    proj_out,
):
    vmem = pl.BlockSpec(memory_space=pltpu.VMEM)
    smem = pl.BlockSpec(memory_space=pltpu.SMEM)
    bf16, f32 = jnp.bfloat16, jnp.float32
    scratch = [
        pltpu.VMEM((10, 128, 128), f32),
        pltpu.VMEM((2, 640, 128), bf16),
        pltpu.VMEM((2, 128, 128), bf16),
        pltpu.VMEM((SLABS, 8, 256), f32),
        pltpu.VMEM((2, SLABS, 128, 256), bf16),
        pltpu.VMEM((SLABS, 128, 256), bf16),
        pltpu.VMEM((2, SLABS, 640, 256), f32),
        pltpu.VMEM((SLABS, 128, 256), f32),
        pltpu.VMEM((SLABS, 8, 256), f32),
        pltpu.VMEM((SLABS, 128, 256), f32),
        pltpu.VMEM((SLABS, 128, 256), f32),
        pltpu.VMEM((SLABS, 128, 256), bf16),
        pltpu.VMEM((SLABS, 128, 256), f32),
        pltpu.VMEM((SLABS, 128, 256), bf16),
        pltpu.VMEM((2048, 128), f32),
        pltpu.VMEM((2048, 128), f32),
        pltpu.VMEM((UNITS, DEVICES, 16, 128), bf16),
        pltpu.VMEM((UNITS, DEVICES, 16, 128), bf16),
        pltpu.SemaphoreType.DMA((UNITS,)),
        pltpu.SemaphoreType.DMA((UNITS,)),
    ]
    shape = jax.ShapeDtypeStruct(pair_in.shape, bf16)
    return pl.pallas_call(
        kernel,
        out_shape=(shape, shape),
        in_specs=[vmem, vmem, smem, smem] + [vmem] * 7,
        out_specs=(vmem, vmem),
        scratch_shapes=scratch,
        compiler_params=pltpu.CompilerParams(
            collective_id=0, has_side_effects=True, vmem_limit_bytes=56 * 1024 * 1024
        ),
    )(
        pair_in,
        grad_out,
        token_valid,
        chain_ids,
        token_valid.reshape(4, 128),
        chain_ids.reshape(4, 128),
        chain_table,
        norm_gain.reshape(4, 128),
        norm_offset.reshape(4, 128),
        proj_in,
        proj_out,
    )


def solution(mesh):
    in_specs = (P("row", "ch", None), P("row", "ch", None), P(), P(), P(), P(), P(), P(), P())
    out_specs = (P("row", "ch", None), P("row", "ch", None))
    return jax.shard_map(local, mesh=mesh, in_specs=in_specs, out_specs=out_specs, check_vma=False)
```

```python
import jax
import jax.numpy as jnp
from jax import lax
from jax.sharding import PartitionSpec as P
from jax.experimental import pallas as pl
from jax.experimental.pallas import tpu as pltpu

EPS = 1e-05
MESH = pl.DeviceIdType.MESH
DEVICES = 128
UNITS = 12
SLABS = 8


def far_first(digit):
    return (digit + 2) - lax.div(digit, 2) * (2 * digit - 1)


def dot(first, second, first_dim=1, second_dim=0):
    return lax.dot_general(
        first,
        second,
        (((first_dim,), (second_dim,)), ((), ())),
        preferred_element_type=jnp.float32,
    )


def normalise(values):
    average = jnp.mean(values, axis=0, keepdims=True)
    centred = values - average
    spread = jnp.mean(centred * centred, axis=0, keepdims=True)
    inverse = lax.rsqrt(spread + EPS)
    return centred * inverse, inverse


def normalise_back(scaled_grad, unit, inverse):
    mean_grad = jnp.mean(scaled_grad, axis=0, keepdims=True)
    mean_prod = jnp.mean(scaled_grad * unit, axis=0, keepdims=True)
    return inverse * (scaled_grad - mean_grad - unit * mean_prod)


def twice(block):
    return jnp.concatenate([block, block], axis=1)


def kernel(
    pair_ref,
    gout_ref,
    valid_s,
    chain_s,
    valid_v,
    chain_v,
    table_ref,
    gain_ref,
    offset_ref,
    win_ref,
    wout_ref,
    final_ref,
    grad_ref,
    par,
    win_t,
    wout_t,
    mask,
    held,
    normed,
    lin,
    unit_t,
    inv_t,
    mixed_s,
    gtn,
    tnorm,
    gnorm,
    upper,
    stage_a,
    stage_b,
    snd,
    rcv,
    ssem,
    rsem,
):
    row, col = lax.axis_index("row"), lax.axis_index("ch")
    z, x = lax.div(row, 8), lax.rem(lax.div(row, 2), 4)
    y, core = lax.div(col, 2) * 2 + lax.rem(row, 2), lax.rem(col, 2)
    me = col * 32 + row

    def partner(t):
        z2 = lax.rem(z + far_first(lax.rem(lax.div(t, 16), 4)), 4)
        x2 = lax.rem(x + far_first(lax.rem(lax.div(t, 4), 4)), 4)
        y2 = lax.rem(y + far_first(lax.rem(t, 4)), 4)
        c2 = lax.rem(core + 1 - lax.div(t, 64), 2)
        return z2 * 8 + x2 * 2 + lax.rem(y2, 2), lax.div(y2, 2) * 2 + c2

    barrier = pltpu.get_barrier_semaphore()

    def greet(t, carry):
        pl.semaphore_signal(barrier, inc=1, device_id=partner(t), device_id_type=MESH)
        return carry

    lax.fori_loop(0, DEVICES - 1, greet, 0)

    def send(u):
        rcv[u, me] = snd[u, me]

        def step(t, carry):
            r2, h2 = partner(t)
            pltpu.make_async_remote_copy(
                src_ref=snd.at[u, h2 * 32 + r2],
                dst_ref=rcv.at[u, me],
                send_sem=ssem.at[u],
                recv_sem=rsem.at[u],
                device_id=(r2, h2),
                device_id_type=MESH,
            ).start()
            return carry

        lax.fori_loop(0, DEVICES - 1, step, 0)

    def whole(u):
        return pltpu.make_async_remote_copy(
            src_ref=snd.at[u, pl.ds(0, DEVICES - 1)],
            dst_ref=rcv.at[u, pl.ds(0, DEVICES - 1)],
            send_sem=ssem.at[u],
            recv_sem=rsem.at[u],
            device_id=(row, col),
            device_id_type=MESH,
        )

    def each_slab(body):
        def step(s, carry):
            body(s)
            return carry

        lax.fori_loop(0, SLABS, step, 0, unroll=4)

    def put(stage, s, value):
        stage[pl.ds(2 * s, 128, stride=16), :] = value[:, :128]
        stage[pl.ds(2 * s + 1, 128, stride=16), :] = value[:, 128:]

    def get(stage, s):
        return jnp.concatenate(
            [stage[pl.ds(2 * s, 128, stride=16), :], stage[pl.ds(2 * s + 1, 128, stride=16), :]],
            axis=1,
        )

    def flush(stage, u):
        def step(q, carry):
            part = stage[pl.ds(pl.multiple_of(q * 256, 256), 256), :]
            snd[u, pl.ds(q * 16, 16)] = part.astype(jnp.bfloat16).reshape(16, 16, 128)
            return carry

        lax.fori_loop(0, 8, step, 0, unroll=4)
        send(u)

    def fetch(u, stage):
        whole(u).wait_recv()

        def step(q, carry):
            part = rcv[u, pl.ds(q * 16, 16)].reshape(256, 128)
            stage[pl.ds(pl.multiple_of(q * 256, 256), 256), :] = part.astype(jnp.float32)
            return carry

        lax.fori_loop(0, 8, step, 0, unroll=4)

    def gain(layer, which):
        return twice(par[2 + 2 * layer + which])

    def offset(layer, which):
        return twice(par[6 + 2 * layer + which])

    def column(row_values):
        return jnp.transpose(jnp.broadcast_to(row_values, (128, 128)))

    def prepare(layer):
        for which in range(2):
            k = 2 * layer + which
            par[2 + k] = column(gain_ref[k : k + 1, :])
            par[6 + k] = column(offset_ref[k : k + 1, :])
        for part in range(5):
            block = win_ref[layer, :, part * 128 : (part + 1) * 128].astype(jnp.float32)
            win_t[layer, part * 128 : (part + 1) * 128, :] = jnp.transpose(block).astype(
                jnp.bfloat16
            )
        wout_t[layer] = jnp.transpose(wout_ref[layer].astype(jnp.float32)).astype(jnp.bfloat16)

    def matrix(u, first=0, count=32):
        return jnp.concatenate(
            [
                rcv[u, 32 * h + first : 32 * h + first + count].reshape(16 * count, 128)
                for h in range(4)
            ],
            axis=1,
        )

    def multiply(u_first, flip_first, u_second, flip_second, u_out):
        second = matrix(u_second)
        for m in range(2):
            if flip_first:
                first = jnp.concatenate(
                    [
                        rcv[u_first, 32 * h : 32 * h + 32].reshape(512, 128)
                        for h in (2 * m, 2 * m + 1)
                    ],
                    axis=1,
                )
            else:
                first = matrix(u_first, 16 * m, 16)
            result = dot(first, second, 0 if flip_first else 1, 1 if flip_second else 0)
            result = result.astype(jnp.bfloat16)
            for h in range(4):
                snd[u_out, 32 * h + 16 * m : 32 * h + 16 * m + 16] = result[
                    :, 128 * h : 128 * h + 128
                ].reshape(16, 16, 128)
        send(u_out)

    def factor(layer, s, part, stage):
        both = dot(win_t[layer, 256 * part : 256 * part + 256, :], normed[s])
        squash = jax.nn.sigmoid(both[:128])
        value = both[128:]
        lin[layer, s, 256 * part : 256 * part + 128, :] = squash
        lin[layer, s, 256 * part + 128 : 256 * part + 256, :] = value
        put(stage, s, mask[s, 0:1, :] * (squash * value))

    def input_norm(layer, s, values):
        unit, _ = normalise(values)
        normed[s] = (unit * gain(layer, 0) + offset(layer, 0)).astype(jnp.bfloat16)

    def open_gate(layer, s):
        lin[layer, s, 512:640, :] = jax.nn.sigmoid(dot(win_t[layer, 512:640, :], normed[s]))

    def product_norm(layer, s, stage):
        unit, inverse = normalise(get(stage, s))
        return unit, inverse, (unit * gain(layer, 1) + offset(layer, 1)).astype(jnp.bfloat16)

    def mixed_back(layer, s, upstream):
        grad_mixed = (upstream * lin[layer, s, 512:640, :]).astype(jnp.bfloat16)
        return dot(wout_ref[layer], grad_mixed)

    def gate_back(layer, s, upstream, mixed):
        gate = lin[layer, s, 512:640, :]
        back = (upstream * mixed * gate * (1.0 - gate)).astype(jnp.bfloat16)
        gnorm[s] = dot(win_ref[layer, :, 512:640], back)

    def factor_back(layer, s, part, stage):
        squash = lin[layer, s, 256 * part : 256 * part + 128, :]
        value = lin[layer, s, 256 * part + 128 : 256 * part + 256, :]
        cotangent = mask[s, 0:1, :] * get(stage, s)
        last = cotangent * squash
        first = last * value * (1.0 - squash)
        both = jnp.concatenate([first.astype(jnp.bfloat16), last.astype(jnp.bfloat16)], axis=0)
        return gnorm[s] + dot(win_ref[layer, :, 256 * part : 256 * part + 256], both)

    def input_back(layer, s, grad_normed):
        unit, inverse = normalise(held[layer, s].astype(jnp.float32))
        back = normalise_back(grad_normed * gain(layer, 0), unit, inverse)
        return (upper[s].astype(jnp.float32) + back).astype(jnp.bfloat16)

    par[0] = column(table_ref[0:1, :])
    par[1] = column(table_ref[1:2, :])
    prepare(0)
    valid_cols = valid_v[pl.ds(col, 1), :].astype(jnp.float32)
    chain_cols = chain_v[pl.ds(col, 1), :]

    def enter(s):
        parts, masks = [], []
        for k in range(2):
            at = row * 16 + 2 * s + k
            masks.append(valid_s[at].astype(jnp.float32) * valid_cols)
            same = (chain_cols == chain_s[at]).astype(jnp.float32)
            block = jnp.transpose(pair_ref[2 * s + k].astype(jnp.float32))
            parts.append(block + same * par[1] + (1.0 - same) * par[0])
        mask[s] = jnp.broadcast_to(jnp.concatenate(masks, axis=1), (8, 256))
        entry = jnp.concatenate(parts, axis=1).astype(jnp.bfloat16)
        held[0, s] = entry
        input_norm(0, s, entry.astype(jnp.float32))
        factor(0, s, 0, stage_a)

    each_slab(enter)
    pl.semaphore_wait(barrier, DEVICES - 1)
    flush(stage_a, 0)
    each_slab(lambda s: factor(0, s, 1, stage_b))
    flush(stage_b, 1)

    def rest_of_entry(s):
        open_gate(0, s)
        parts = [jnp.transpose(gout_ref[2 * s + k].astype(jnp.float32)) for k in range(2)]
        upper[s] = jnp.concatenate(parts, axis=1).astype(jnp.bfloat16)

    each_slab(rest_of_entry)
    prepare(1)
    whole(0).wait_recv()
    whole(1).wait_recv()
    multiply(0, False, 1, True, 2)

    fetch(2, stage_a)

    def middle(s):
        unit, inverse, scaled = product_norm(0, s, stage_a)
        unit_t[s] = unit
        inv_t[s] = jnp.broadcast_to(inverse, (8, 256))
        mixed = dot(wout_t[0], scaled)
        mixed_s[s] = mixed
        value = held[0, s].astype(jnp.float32) + lin[0, s, 512:640, :] * mixed
        value = value.astype(jnp.bfloat16)
        held[1, s] = value
        input_norm(1, s, value.astype(jnp.float32))
        factor(1, s, 0, stage_b)

    each_slab(middle)
    flush(stage_b, 3)
    each_slab(lambda s: factor(1, s, 1, stage_a))
    flush(stage_a, 4)

    def rest_of_middle(s):
        open_gate(1, s)
        gtn[s] = mixed_back(1, s, upper[s].astype(jnp.float32))

    each_slab(rest_of_middle)
    whole(3).wait_recv()
    whole(4).wait_recv()
    multiply(3, True, 4, False, 5)

    fetch(5, stage_a)

    def turn(s):
        unit, inverse, scaled = product_norm(1, s, stage_a)
        tnorm[s] = scaled
        put(stage_b, s, normalise_back(gtn[s] * gain(1, 1), unit, inverse))

    each_slab(turn)
    flush(stage_b, 6)

    def finish(s):
        mixed = dot(wout_t[1], tnorm[s])
        value = held[1, s].astype(jnp.float32) + lin[1, s, 512:640, :] * mixed
        for k in range(2):
            final_ref[2 * s + k] = jnp.transpose(value[:, 128 * k : 128 * k + 128]).astype(
                jnp.bfloat16
            )
        gate_back(1, s, upper[s].astype(jnp.float32), mixed)

    each_slab(finish)
    whole(6).wait_recv()
    multiply(4, False, 6, True, 7)
    multiply(3, False, 6, False, 8)
    fetch(7, stage_a)

    def left_back(layer, s):
        gnorm[s] = factor_back(layer, s, 0, stage_a)

    each_slab(lambda s: left_back(1, s))
    fetch(8, stage_b)

    def lower(s):
        value = input_back(1, s, factor_back(1, s, 1, stage_b))
        upper[s] = value
        grad_tnorm = mixed_back(0, s, value.astype(jnp.float32))
        put(stage_a, s, normalise_back(grad_tnorm * gain(0, 1), unit_t[s], inv_t[s, 0:1, :]))

    each_slab(lower)
    flush(stage_a, 9)
    each_slab(lambda s: gate_back(0, s, upper[s].astype(jnp.float32), mixed_s[s]))
    whole(9).wait_recv()
    multiply(9, False, 1, False, 10)
    multiply(9, True, 0, False, 11)
    fetch(10, stage_a)
    each_slab(lambda s: left_back(0, s))
    fetch(11, stage_b)

    def leave(s):
        value = input_back(0, s, factor_back(0, s, 1, stage_b)).astype(jnp.float32)
        for k in range(2):
            grad_ref[2 * s + k] = jnp.transpose(value[:, 128 * k : 128 * k + 128]).astype(
                jnp.bfloat16
            )

    each_slab(leave)
    for u in range(UNITS):
        whole(u).wait_send()


def local(
    pair_in,
    grad_out,
    token_valid,
    chain_ids,
    chain_table,
    norm_gain,
    norm_offset,
    proj_in,
    proj_out,
):
    vmem = pl.BlockSpec(memory_space=pltpu.VMEM)
    smem = pl.BlockSpec(memory_space=pltpu.SMEM)
    bf16, f32 = jnp.bfloat16, jnp.float32
    scratch = [
        pltpu.VMEM((10, 128, 128), f32),
        pltpu.VMEM((2, 640, 128), bf16),
        pltpu.VMEM((2, 128, 128), bf16),
        pltpu.VMEM((SLABS, 8, 256), f32),
        pltpu.VMEM((2, SLABS, 128, 256), bf16),
        pltpu.VMEM((SLABS, 128, 256), bf16),
        pltpu.VMEM((2, SLABS, 640, 256), f32),
        pltpu.VMEM((SLABS, 128, 256), f32),
        pltpu.VMEM((SLABS, 8, 256), f32),
        pltpu.VMEM((SLABS, 128, 256), f32),
        pltpu.VMEM((SLABS, 128, 256), f32),
        pltpu.VMEM((SLABS, 128, 256), bf16),
        pltpu.VMEM((SLABS, 128, 256), f32),
        pltpu.VMEM((SLABS, 128, 256), bf16),
        pltpu.VMEM((2048, 128), f32),
        pltpu.VMEM((2048, 128), f32),
        pltpu.VMEM((UNITS, DEVICES, 16, 128), bf16),
        pltpu.VMEM((UNITS, DEVICES, 16, 128), bf16),
        pltpu.SemaphoreType.DMA((UNITS,)),
        pltpu.SemaphoreType.DMA((UNITS,)),
    ]
    shape = jax.ShapeDtypeStruct(pair_in.shape, bf16)
    return pl.pallas_call(
        kernel,
        out_shape=(shape, shape),
        in_specs=[vmem, vmem, smem, smem] + [vmem] * 7,
        out_specs=(vmem, vmem),
        scratch_shapes=scratch,
        compiler_params=pltpu.CompilerParams(
            collective_id=0, has_side_effects=True, vmem_limit_bytes=56 * 1024 * 1024
        ),
    )(
        pair_in,
        grad_out,
        token_valid,
        chain_ids,
        token_valid.reshape(4, 128),
        chain_ids.reshape(4, 128),
        chain_table,
        norm_gain.reshape(4, 128),
        norm_offset.reshape(4, 128),
        proj_in,
        proj_out,
    )


def solution(mesh):
    in_specs = (P("row", "ch", None), P("row", "ch", None), P(), P(), P(), P(), P(), P(), P())
    out_specs = (P("row", "ch", None), P("row", "ch", None))
    return jax.shard_map(local, mesh=mesh, in_specs=in_specs, out_specs=out_specs, check_vma=False)
```

```python
import jax
import jax.numpy as jnp
from jax import lax
from jax.sharding import PartitionSpec as P
from jax.experimental import pallas as pl
from jax.experimental.pallas import tpu as pltpu

EPS = 1e-05
MESH = pl.DeviceIdType.MESH
DEVICES = 128
UNITS = 12
FAR_FIRST = (2, 3, 1, 0)
SLABS = 8


def far_first(digit):
    return (digit + 2) - lax.div(digit, 2) * (2 * digit - 1)


def dot(first, second, first_dim=1, second_dim=0):
    return lax.dot_general(
        first,
        second,
        (((first_dim,), (second_dim,)), ((), ())),
        preferred_element_type=jnp.float32,
    )


def normalise(values):
    average = jnp.mean(values, axis=0, keepdims=True)
    centred = values - average
    spread = jnp.mean(centred * centred, axis=0, keepdims=True)
    inverse = lax.rsqrt(spread + EPS)
    return centred * inverse, inverse


def normalise_back(scaled_grad, unit, inverse):
    mean_grad = jnp.mean(scaled_grad, axis=0, keepdims=True)
    mean_prod = jnp.mean(scaled_grad * unit, axis=0, keepdims=True)
    return inverse * (scaled_grad - mean_grad - unit * mean_prod)


def twice(block):
    return jnp.concatenate([block, block], axis=1)


def kernel(
    pair_ref,
    gout_ref,
    valid_s,
    chain_s,
    valid_v,
    chain_v,
    table_ref,
    gain_ref,
    offset_ref,
    win_ref,
    wout_ref,
    final_ref,
    grad_ref,
    par,
    win_t,
    wout_t,
    mask,
    held,
    normed,
    lin,
    unit_t,
    inv_t,
    mixed_s,
    gtn,
    tnorm,
    gnorm,
    upper,
    stage_a,
    stage_b,
    snd,
    rcv,
    ssem,
    rsem,
):
    row, col = lax.axis_index("row"), lax.axis_index("ch")
    z, x = lax.div(row, 8), lax.rem(lax.div(row, 2), 4)
    y, core = lax.div(col, 2) * 2 + lax.rem(row, 2), lax.rem(col, 2)
    me = col * 32 + row

    xs = [lax.rem(x + q, 4) * 2 for q in FAR_FIRST]
    ys = [lax.rem(y + q, 4) for q in FAR_FIRST]
    ys = [(lax.rem(value, 2), lax.div(value, 2) * 2) for value in ys]
    spots = [(x_part + low, high) for x_part in xs for low, high in ys]

    def each_partner(act):
        def step(t, carry):
            r2 = lax.rem(z + far_first(lax.rem(t, 4)), 4) * 8
            h2 = lax.rem(core + 1 - lax.div(t, 4), 2)
            for r_part, h_part in spots:
                act(r2 + r_part, h2 + h_part)
            return carry

        lax.fori_loop(0, 7, step, 0)
        for r_part, h_part in spots[:-1]:
            act(z * 8 + r_part, core + h_part)

    barrier = pltpu.get_barrier_semaphore()
    each_partner(
        lambda r2, h2: pl.semaphore_signal(
            barrier, inc=1, device_id=(r2, h2), device_id_type=MESH
        )
    )

    def send(u):
        rcv[u, me] = snd[u, me]
        each_partner(
            lambda r2, h2: pltpu.make_async_remote_copy(
                src_ref=snd.at[u, h2 * 32 + r2],
                dst_ref=rcv.at[u, me],
                send_sem=ssem.at[u],
                recv_sem=rsem.at[u],
                device_id=(r2, h2),
                device_id_type=MESH,
            ).start()
        )

    def whole(u):
        return pltpu.make_async_remote_copy(
            src_ref=snd.at[u, pl.ds(0, DEVICES - 1)],
            dst_ref=rcv.at[u, pl.ds(0, DEVICES - 1)],
            send_sem=ssem.at[u],
            recv_sem=rsem.at[u],
            device_id=(row, col),
            device_id_type=MESH,
        )

    def each_slab(body):
        def step(s, carry):
            body(s)
            return carry

        lax.fori_loop(0, SLABS, step, 0, unroll=8)

    def put(stage, s, value):
        stage[pl.ds(2 * s, 128, stride=16), :] = value[:, :128]
        stage[pl.ds(2 * s + 1, 128, stride=16), :] = value[:, 128:]

    def get(stage, s):
        return jnp.concatenate(
            [stage[pl.ds(2 * s, 128, stride=16), :], stage[pl.ds(2 * s + 1, 128, stride=16), :]],
            axis=1,
        )

    def flush(stage, u):
        def step(q, carry):
            part = stage[pl.ds(pl.multiple_of(q * 256, 256), 256), :]
            snd[u, pl.ds(q * 16, 16)] = part.astype(jnp.bfloat16).reshape(16, 16, 128)
            return carry

        lax.fori_loop(0, 8, step, 0, unroll=8)
        send(u)

    def fetch(u, stage):
        whole(u).wait_recv()

        def step(q, carry):
            part = rcv[u, pl.ds(q * 16, 16)].reshape(256, 128)
            stage[pl.ds(pl.multiple_of(q * 256, 256), 256), :] = part.astype(jnp.float32)
            return carry

        lax.fori_loop(0, 8, step, 0, unroll=8)

    def gain(layer, which):
        return twice(par[2 + 2 * layer + which])

    def offset(layer, which):
        return twice(par[6 + 2 * layer + which])

    def column(row_values):
        return jnp.transpose(jnp.broadcast_to(row_values, (128, 128)))

    def prepare(layer):
        for which in range(2):
            k = 2 * layer + which
            par[2 + k] = column(gain_ref[k : k + 1, :])
            par[6 + k] = column(offset_ref[k : k + 1, :])
        for part in range(5):
            block = win_ref[layer, :, part * 128 : (part + 1) * 128].astype(jnp.float32)
            win_t[layer, part * 128 : (part + 1) * 128, :] = jnp.transpose(block).astype(
                jnp.bfloat16
            )
        wout_t[layer] = jnp.transpose(wout_ref[layer].astype(jnp.float32)).astype(jnp.bfloat16)

    def matrix(u, first=0, count=32):
        return jnp.concatenate(
            [
                rcv[u, 32 * h + first : 32 * h + first + count].reshape(16 * count, 128)
                for h in range(4)
            ],
            axis=1,
        )

    def multiply(u_first, flip_first, u_second, flip_second, u_out):
        second = matrix(u_second)
        for m in range(2):
            if flip_first:
                first = jnp.concatenate(
                    [
                        rcv[u_first, 32 * h : 32 * h + 32].reshape(512, 128)
                        for h in (2 * m, 2 * m + 1)
                    ],
                    axis=1,
                )
            else:
                first = matrix(u_first, 16 * m, 16)
            result = dot(first, second, 0 if flip_first else 1, 1 if flip_second else 0)
            result = result.astype(jnp.bfloat16)
            for h in range(4):
                snd[u_out, 32 * h + 16 * m : 32 * h + 16 * m + 16] = result[
                    :, 128 * h : 128 * h + 128
                ].reshape(16, 16, 128)
        send(u_out)

    def factor(layer, s, part, stage):
        both = dot(win_t[layer, 256 * part : 256 * part + 256, :], normed[s])
        squash = jax.nn.sigmoid(both[:128])
        value = both[128:]
        lin[layer, s, 256 * part : 256 * part + 128, :] = squash
        lin[layer, s, 256 * part + 128 : 256 * part + 256, :] = value
        put(stage, s, mask[s, 0:1, :] * (squash * value))

    def input_norm(layer, s, values):
        unit, _ = normalise(values)
        normed[s] = (unit * gain(layer, 0) + offset(layer, 0)).astype(jnp.bfloat16)

    def open_gate(layer, s):
        lin[layer, s, 512:640, :] = jax.nn.sigmoid(dot(win_t[layer, 512:640, :], normed[s]))

    def product_norm(layer, s, stage):
        unit, inverse = normalise(get(stage, s))
        return unit, inverse, (unit * gain(layer, 1) + offset(layer, 1)).astype(jnp.bfloat16)

    def mixed_back(layer, s, upstream):
        grad_mixed = (upstream * lin[layer, s, 512:640, :]).astype(jnp.bfloat16)
        return dot(wout_ref[layer], grad_mixed)

    def gate_back(layer, s, upstream, mixed):
        gate = lin[layer, s, 512:640, :]
        back = (upstream * mixed * gate * (1.0 - gate)).astype(jnp.bfloat16)
        gnorm[s] = dot(win_ref[layer, :, 512:640], back)

    def factor_back(layer, s, part, stage):
        squash = lin[layer, s, 256 * part : 256 * part + 128, :]
        value = lin[layer, s, 256 * part + 128 : 256 * part + 256, :]
        cotangent = mask[s, 0:1, :] * get(stage, s)
        last = cotangent * squash
        first = last * value * (1.0 - squash)
        both = jnp.concatenate([first.astype(jnp.bfloat16), last.astype(jnp.bfloat16)], axis=0)
        return gnorm[s] + dot(win_ref[layer, :, 256 * part : 256 * part + 256], both)

    def input_back(layer, s, grad_normed):
        unit, inverse = normalise(held[layer, s].astype(jnp.float32))
        back = normalise_back(grad_normed * gain(layer, 0), unit, inverse)
        return (upper[s].astype(jnp.float32) + back).astype(jnp.bfloat16)

    par[0] = column(table_ref[0:1, :])
    par[1] = column(table_ref[1:2, :])
    prepare(0)
    valid_cols = valid_v[pl.ds(col, 1), :].astype(jnp.float32)
    chain_cols = chain_v[pl.ds(col, 1), :]

    def enter(s):
        parts, masks = [], []
        for k in range(2):
            at = row * 16 + 2 * s + k
            masks.append(valid_s[at].astype(jnp.float32) * valid_cols)
            same = (chain_cols == chain_s[at]).astype(jnp.float32)
            block = jnp.transpose(pair_ref[2 * s + k].astype(jnp.float32))
            parts.append(block + same * par[1] + (1.0 - same) * par[0])
        mask[s] = jnp.broadcast_to(jnp.concatenate(masks, axis=1), (8, 256))
        entry = jnp.concatenate(parts, axis=1).astype(jnp.bfloat16)
        held[0, s] = entry
        input_norm(0, s, entry.astype(jnp.float32))
        factor(0, s, 0, stage_a)

    each_slab(enter)
    pl.semaphore_wait(barrier, DEVICES - 1)
    flush(stage_a, 0)
    each_slab(lambda s: factor(0, s, 1, stage_b))
    flush(stage_b, 1)

    def rest_of_entry(s):
        open_gate(0, s)
        parts = [jnp.transpose(gout_ref[2 * s + k].astype(jnp.float32)) for k in range(2)]
        upper[s] = jnp.concatenate(parts, axis=1).astype(jnp.bfloat16)

    each_slab(rest_of_entry)
    prepare(1)
    whole(0).wait_recv()
    whole(1).wait_recv()
    multiply(0, False, 1, True, 2)

    fetch(2, stage_a)

    def middle(s):
        unit, inverse, scaled = product_norm(0, s, stage_a)
        unit_t[s] = unit
        inv_t[s] = jnp.broadcast_to(inverse, (8, 256))
        mixed = dot(wout_t[0], scaled)
        mixed_s[s] = mixed
        value = held[0, s].astype(jnp.float32) + lin[0, s, 512:640, :] * mixed
        value = value.astype(jnp.bfloat16)
        held[1, s] = value
        input_norm(1, s, value.astype(jnp.float32))
        factor(1, s, 0, stage_b)

    each_slab(middle)
    flush(stage_b, 3)
    each_slab(lambda s: factor(1, s, 1, stage_a))
    flush(stage_a, 4)

    def rest_of_middle(s):
        open_gate(1, s)
        gtn[s] = mixed_back(1, s, upper[s].astype(jnp.float32))

    each_slab(rest_of_middle)
    whole(3).wait_recv()
    whole(4).wait_recv()
    multiply(3, True, 4, False, 5)

    fetch(5, stage_a)

    def turn(s):
        unit, inverse, scaled = product_norm(1, s, stage_a)
        tnorm[s] = scaled
        put(stage_b, s, normalise_back(gtn[s] * gain(1, 1), unit, inverse))

    each_slab(turn)
    flush(stage_b, 6)

    def finish(s):
        mixed = dot(wout_t[1], tnorm[s])
        value = held[1, s].astype(jnp.float32) + lin[1, s, 512:640, :] * mixed
        for k in range(2):
            final_ref[2 * s + k] = jnp.transpose(value[:, 128 * k : 128 * k + 128]).astype(
                jnp.bfloat16
            )
        gate_back(1, s, upper[s].astype(jnp.float32), mixed)

    each_slab(finish)
    whole(6).wait_recv()
    multiply(4, False, 6, True, 7)
    multiply(3, False, 6, False, 8)
    fetch(7, stage_a)

    def left_back(layer, s):
        gnorm[s] = factor_back(layer, s, 0, stage_a)

    each_slab(lambda s: left_back(1, s))
    fetch(8, stage_b)

    def lower(s):
        value = input_back(1, s, factor_back(1, s, 1, stage_b))
        upper[s] = value
        grad_tnorm = mixed_back(0, s, value.astype(jnp.float32))
        put(stage_a, s, normalise_back(grad_tnorm * gain(0, 1), unit_t[s], inv_t[s, 0:1, :]))

    each_slab(lower)
    flush(stage_a, 9)
    each_slab(lambda s: gate_back(0, s, upper[s].astype(jnp.float32), mixed_s[s]))
    whole(9).wait_recv()
    multiply(9, False, 1, False, 10)
    multiply(9, True, 0, False, 11)
    fetch(10, stage_a)
    each_slab(lambda s: left_back(0, s))
    fetch(11, stage_b)

    def leave(s):
        value = input_back(0, s, factor_back(0, s, 1, stage_b)).astype(jnp.float32)
        for k in range(2):
            grad_ref[2 * s + k] = jnp.transpose(value[:, 128 * k : 128 * k + 128]).astype(
                jnp.bfloat16
            )

    each_slab(leave)
    for u in range(UNITS):
        whole(u).wait_send()


def local(
    pair_in,
    grad_out,
    token_valid,
    chain_ids,
    chain_table,
    norm_gain,
    norm_offset,
    proj_in,
    proj_out,
):
    vmem = pl.BlockSpec(memory_space=pltpu.VMEM)
    smem = pl.BlockSpec(memory_space=pltpu.SMEM)
    bf16, f32 = jnp.bfloat16, jnp.float32
    scratch = [
        pltpu.VMEM((10, 128, 128), f32),
        pltpu.VMEM((2, 640, 128), bf16),
        pltpu.VMEM((2, 128, 128), bf16),
        pltpu.VMEM((SLABS, 8, 256), f32),
        pltpu.VMEM((2, SLABS, 128, 256), bf16),
        pltpu.VMEM((SLABS, 128, 256), bf16),
        pltpu.VMEM((2, SLABS, 640, 256), f32),
        pltpu.VMEM((SLABS, 128, 256), f32),
        pltpu.VMEM((SLABS, 8, 256), f32),
        pltpu.VMEM((SLABS, 128, 256), f32),
        pltpu.VMEM((SLABS, 128, 256), f32),
        pltpu.VMEM((SLABS, 128, 256), bf16),
        pltpu.VMEM((SLABS, 128, 256), f32),
        pltpu.VMEM((SLABS, 128, 256), bf16),
        pltpu.VMEM((2048, 128), f32),
        pltpu.VMEM((2048, 128), f32),
        pltpu.VMEM((UNITS, DEVICES, 16, 128), bf16),
        pltpu.VMEM((UNITS, DEVICES, 16, 128), bf16),
        pltpu.SemaphoreType.DMA((UNITS,)),
        pltpu.SemaphoreType.DMA((UNITS,)),
    ]
    shape = jax.ShapeDtypeStruct(pair_in.shape, bf16)
    return pl.pallas_call(
        kernel,
        out_shape=(shape, shape),
        in_specs=[vmem, vmem, smem, smem] + [vmem] * 7,
        out_specs=(vmem, vmem),
        scratch_shapes=scratch,
        compiler_params=pltpu.CompilerParams(
            collective_id=0, has_side_effects=True, vmem_limit_bytes=56 * 1024 * 1024
        ),
    )(
        pair_in,
        grad_out,
        token_valid,
        chain_ids,
        token_valid.reshape(4, 128),
        chain_ids.reshape(4, 128),
        chain_table,
        norm_gain.reshape(4, 128),
        norm_offset.reshape(4, 128),
        proj_in,
        proj_out,
    )


def solution(mesh):
    in_specs = (P("row", "ch", None), P("row", "ch", None), P(), P(), P(), P(), P(), P(), P())
    out_specs = (P("row", "ch", None), P("row", "ch", None))
    return jax.shard_map(local, mesh=mesh, in_specs=in_specs, out_specs=out_specs, check_vma=False)
```

```python
import jax
import jax.numpy as jnp
from jax import lax
from jax.sharding import PartitionSpec as P
from jax.experimental import pallas as pl
from jax.experimental.pallas import tpu as pltpu

EPS = 1e-05
MESH = pl.DeviceIdType.MESH
DEVICES = 128
UNITS = 12
FAR_FIRST = (2, 3, 1, 0)
SLABS = 8


def far_first(digit):
    return (digit + 2) - lax.div(digit, 2) * (2 * digit - 1)


def dot(first, second, first_dim=1, second_dim=0):
    return lax.dot_general(
        first,
        second,
        (((first_dim,), (second_dim,)), ((), ())),
        preferred_element_type=jnp.float32,
    )


def normalise(values):
    average = jnp.mean(values, axis=0, keepdims=True)
    centred = values - average
    spread = jnp.mean(centred * centred, axis=0, keepdims=True)
    inverse = lax.rsqrt(spread + EPS)
    return centred * inverse, inverse


def normalise_back(scaled_grad, unit, inverse):
    mean_grad = jnp.mean(scaled_grad, axis=0, keepdims=True)
    mean_prod = jnp.mean(scaled_grad * unit, axis=0, keepdims=True)
    return inverse * (scaled_grad - mean_grad - unit * mean_prod)


def twice(block):
    return jnp.concatenate([block, block], axis=1)


def kernel(
    pair_ref,
    gout_ref,
    valid_s,
    chain_s,
    valid_v,
    chain_v,
    table_ref,
    gain_ref,
    offset_ref,
    win_ref,
    wout_ref,
    final_ref,
    grad_ref,
    par,
    win_t,
    wout_t,
    mask,
    held,
    normed,
    lin,
    unit_t,
    inv_t,
    mixed_s,
    gtn,
    tnorm,
    gnorm,
    upper,
    stage_a,
    stage_b,
    snd,
    rcv,
    ssem,
    rsem,
):
    row, col = lax.axis_index("row"), lax.axis_index("ch")
    z, x = lax.div(row, 8), lax.rem(lax.div(row, 2), 4)
    y, core = lax.div(col, 2) * 2 + lax.rem(row, 2), lax.rem(col, 2)
    me = col * 32 + row

    xs = [lax.rem(x + q, 4) * 2 for q in FAR_FIRST]
    ys = [lax.rem(y + q, 4) for q in FAR_FIRST]
    ys = [(lax.rem(value, 2), lax.div(value, 2) * 2) for value in ys]
    spots = [(x_part + low, high) for x_part in xs for low, high in ys]

    def by_core(t):
        plane = lax.rem(z + far_first(lax.rem(t, 4)), 4)
        return plane, lax.rem(core + 1 - lax.div(t, 4), 2), lax.div(t, 4)

    def by_half(t):
        plane = lax.rem(z + far_first(2 * lax.div(t, 4) + lax.rem(t, 2)), 4)
        return plane, lax.rem(core + 1 - lax.rem(lax.div(t, 2), 2), 2), lax.div(t, 4)

    def to_each(act, order, first, count, with_self):
        def step(t, carry):
            plane, core2, part = order(t)
            for r_part, h_part in spots:
                act(plane * 8 + r_part, core2 + h_part, part)
            return carry

        lax.fori_loop(first, first + count - (1 if with_self else 0), step, 0)
        if with_self:
            part = order(jnp.int32(first + count - 1))[2]
            for r_part, h_part in spots[:-1]:
                act(z * 8 + r_part, core + h_part, part)

    barrier = pltpu.get_barrier_semaphore()
    to_each(
        lambda r2, h2, part: pl.semaphore_signal(
            barrier, inc=1, device_id=(r2, h2), device_id_type=MESH
        ),
        by_core,
        0,
        8,
        True,
    )

    def copy_to(u, split):
        def act(r2, h2, part):
            pltpu.make_async_remote_copy(
                src_ref=snd.at[u, h2 * 32 + r2],
                dst_ref=rcv.at[u, me],
                send_sem=ssem.at[u],
                recv_sem=rsem.at[u, part if split else 0],
                device_id=(r2, h2),
                device_id_type=MESH,
            ).start()

        return act

    def keep(u):
        rcv[u, me] = snd[u, me]

    def send(u, split=False, order=by_core):
        keep(u)
        to_each(copy_to(u, split), order, 0, 8, True)

    def whole(u, part=0, count=DEVICES - 1):
        return pltpu.make_async_remote_copy(
            src_ref=snd.at[u, pl.ds(0, count)],
            dst_ref=rcv.at[u, pl.ds(0, count)],
            send_sem=ssem.at[u],
            recv_sem=rsem.at[u, part],
            device_id=(row, col),
            device_id_type=MESH,
        )

    def wait_part(u, part):
        whole(u, part, 64 - part).wait_recv()

    def each_slab(body):
        def step(s, carry):
            body(s)
            return carry

        lax.fori_loop(0, SLABS, step, 0, unroll=8)

    def put(stage, s, value):
        stage[pl.ds(2 * s, 128, stride=16), :] = value[:, :128]
        stage[pl.ds(2 * s + 1, 128, stride=16), :] = value[:, 128:]

    def get(stage, s):
        return jnp.concatenate(
            [stage[pl.ds(2 * s, 128, stride=16), :], stage[pl.ds(2 * s + 1, 128, stride=16), :]],
            axis=1,
        )

    def flush(stage, u, split=False, order=by_core):
        def step(q, carry):
            part = stage[pl.ds(pl.multiple_of(q * 256, 256), 256), :]
            snd[u, pl.ds(q * 16, 16)] = part.astype(jnp.bfloat16).reshape(16, 16, 128)
            return carry

        lax.fori_loop(0, 8, step, 0, unroll=8)
        send(u, split, order)

    def fetch(u, stage):
        whole(u).wait_recv()

        def step(q, carry):
            part = rcv[u, pl.ds(q * 16, 16)].reshape(256, 128)
            stage[pl.ds(pl.multiple_of(q * 256, 256), 256), :] = part.astype(jnp.float32)
            return carry

        lax.fori_loop(0, 8, step, 0, unroll=8)

    def gain(layer, which):
        return twice(par[2 + 2 * layer + which])

    def offset(layer, which):
        return twice(par[6 + 2 * layer + which])

    def column(row_values):
        return jnp.transpose(jnp.broadcast_to(row_values, (128, 128)))

    def prepare(layer):
        for which in range(2):
            k = 2 * layer + which
            par[2 + k] = column(gain_ref[k : k + 1, :])
            par[6 + k] = column(offset_ref[k : k + 1, :])
        for part in range(5):
            block = win_ref[layer, :, part * 128 : (part + 1) * 128].astype(jnp.float32)
            win_t[layer, part * 128 : (part + 1) * 128, :] = jnp.transpose(block).astype(
                jnp.bfloat16
            )
        wout_t[layer] = jnp.transpose(wout_ref[layer].astype(jnp.float32)).astype(jnp.bfloat16)

    def matrix(u, first=0, count=32):
        return jnp.concatenate(
            [
                rcv[u, 32 * h + first : 32 * h + first + count].reshape(16 * count, 128)
                for h in range(4)
            ],
            axis=1,
        )

    def column_of(u, h):
        return rcv[u, pl.ds(32 * h, 32)].reshape(512, 128)

    def plane_rows(u, plane):
        return jnp.concatenate(
            [rcv[u, pl.ds(32 * h + 8 * plane, 8)].reshape(128, 128) for h in range(4)], axis=1
        )

    def store_rows(u, plane, result):
        result = result.astype(jnp.bfloat16)
        for h in range(4):
            part = result[:, 128 * h : 128 * h + 128]
            snd[u, pl.ds(32 * h + 8 * plane, 8)] = part.reshape(8, 16, 128)

    def multiply(u_first, u_second, flip_second, u_out):
        second = matrix(u_second)
        for m in range(2):
            result = dot(matrix(u_first, 16 * m, 16), second, 1, 1 if flip_second else 0)
            result = result.astype(jnp.bfloat16)
            for h in range(4):
                snd[u_out, 32 * h + 16 * m : 32 * h + 16 * m + 16] = result[
                    :, 128 * h : 128 * h + 128
                ].reshape(16, 16, 128)
        send(u_out)

    def rows_by_half(u_first, u_second, u_out):
        second = matrix(u_second)
        for part in range(2):
            wait_part(u_first, part)
            planes = [lax.rem(z + 4 - FAR_FIRST[2 * part + k], 4) for k in range(2)]
            both = jnp.concatenate([plane_rows(u_first, plane) for plane in planes], axis=0)
            result = dot(both, second, 1, 1)
            for k in range(2):
                store_rows(u_out, planes[k], result[128 * k : 128 * k + 128])

            def order(t):
                step = 3 - 3 * lax.rem(t, 2) if part else 2 - lax.rem(t, 2)
                return lax.rem(z + step, 4), lax.rem(core + 1 - lax.div(t, 2), 2), 0

            if part:
                keep(u_out)
            to_each(copy_to(u_out, False), order, 0, 4, part == 1)

    def rows_by_core(u_first, u_second, u_out):
        second = matrix(u_second)
        act = copy_to(u_out, False)
        for part in range(2):
            wait_part(u_first, part)
            own = lax.rem(core + 1 - part, 2)
            planes = [own, own + 2]
            both = jnp.concatenate([column_of(u_first, h) for h in planes], axis=1)
            result = dot(both, second, 0, 0)
            for k in range(2):
                store_rows(u_out, planes[k], result[128 * k : 128 * k + 128])

            def step(t, carry):
                plane = own + 2 * lax.rem(t, 2)
                core2 = lax.rem(core + 1 - lax.div(t, 2), 2)
                for r_part, h_part in spots[:-1]:
                    act(plane * 8 + r_part, core2 + h_part, 0)
                r_part, h_part = spots[-1]

                @pl.when(jnp.logical_or(plane != z, core2 != core))
                def _():
                    act(plane * 8 + r_part, core2 + h_part, 0)

                return carry

            lax.fori_loop(0, 4, step, 0)
        keep(u_out)

    def columns_by_core(u_first, u_second, u_out):
        first = matrix(u_first)
        for part in range(2):
            wait_part(u_second, part)
            own = lax.rem(core + 1 - part, 2)
            columns = [own, own + 2]
            both = jnp.concatenate([column_of(u_second, h) for h in columns], axis=1)
            result = dot(first, both, 1, 0).astype(jnp.bfloat16)
            for k in range(2):
                block = result[:, 128 * k : 128 * k + 128]
                snd[u_out, pl.ds(32 * columns[k], 32)] = block.reshape(32, 16, 128)
            if part:
                keep(u_out)
            to_each(copy_to(u_out, False), by_core, 4 * part, 4, part == 1)

    def factor(layer, s, part, stage):
        both = dot(win_t[layer, 256 * part : 256 * part + 256, :], normed[s])
        squash = jax.nn.sigmoid(both[:128])
        value = both[128:]
        lin[layer, s, 256 * part : 256 * part + 128, :] = squash
        lin[layer, s, 256 * part + 128 : 256 * part + 256, :] = value
        put(stage, s, mask[s, 0:1, :] * (squash * value))

    def input_norm(layer, s, values):
        unit, _ = normalise(values)
        normed[s] = (unit * gain(layer, 0) + offset(layer, 0)).astype(jnp.bfloat16)

    def open_gate(layer, s):
        lin[layer, s, 512:640, :] = jax.nn.sigmoid(dot(win_t[layer, 512:640, :], normed[s]))

    def product_norm(layer, s, stage):
        unit, inverse = normalise(get(stage, s))
        return unit, inverse, (unit * gain(layer, 1) + offset(layer, 1)).astype(jnp.bfloat16)

    def mixed_back(layer, s, upstream):
        grad_mixed = (upstream * lin[layer, s, 512:640, :]).astype(jnp.bfloat16)
        return dot(wout_ref[layer], grad_mixed)

    def gate_back(layer, s, upstream, mixed):
        gate = lin[layer, s, 512:640, :]
        back = (upstream * mixed * gate * (1.0 - gate)).astype(jnp.bfloat16)
        gnorm[s] = dot(win_ref[layer, :, 512:640], back)

    def factor_back(layer, s, part, stage):
        squash = lin[layer, s, 256 * part : 256 * part + 128, :]
        value = lin[layer, s, 256 * part + 128 : 256 * part + 256, :]
        cotangent = mask[s, 0:1, :] * get(stage, s)
        last = cotangent * squash
        first = last * value * (1.0 - squash)
        both = jnp.concatenate([first.astype(jnp.bfloat16), last.astype(jnp.bfloat16)], axis=0)
        return gnorm[s] + dot(win_ref[layer, :, 256 * part : 256 * part + 256], both)

    def input_back(layer, s, grad_normed):
        unit, inverse = normalise(held[layer, s].astype(jnp.float32))
        back = normalise_back(grad_normed * gain(layer, 0), unit, inverse)
        return (upper[s].astype(jnp.float32) + back).astype(jnp.bfloat16)

    par[0] = column(table_ref[0:1, :])
    par[1] = column(table_ref[1:2, :])
    prepare(0)
    valid_cols = valid_v[pl.ds(col, 1), :].astype(jnp.float32)
    chain_cols = chain_v[pl.ds(col, 1), :]

    def enter(s):
        parts, masks = [], []
        for k in range(2):
            at = row * 16 + 2 * s + k
            masks.append(valid_s[at].astype(jnp.float32) * valid_cols)
            same = (chain_cols == chain_s[at]).astype(jnp.float32)
            block = jnp.transpose(pair_ref[2 * s + k].astype(jnp.float32))
            parts.append(block + same * par[1] + (1.0 - same) * par[0])
        mask[s] = jnp.broadcast_to(jnp.concatenate(masks, axis=1), (8, 256))
        entry = jnp.concatenate(parts, axis=1).astype(jnp.bfloat16)
        held[0, s] = entry
        input_norm(0, s, entry.astype(jnp.float32))
        factor(0, s, 0, stage_a)

    each_slab(enter)
    pl.semaphore_wait(barrier, DEVICES - 1)
    flush(stage_a, 0)
    each_slab(lambda s: factor(0, s, 1, stage_b))
    flush(stage_b, 1)

    def rest_of_entry(s):
        open_gate(0, s)
        parts = [jnp.transpose(gout_ref[2 * s + k].astype(jnp.float32)) for k in range(2)]
        upper[s] = jnp.concatenate(parts, axis=1).astype(jnp.bfloat16)

    each_slab(rest_of_entry)
    prepare(1)
    whole(0).wait_recv()
    whole(1).wait_recv()
    multiply(0, 1, True, 2)

    fetch(2, stage_a)

    def middle(s):
        unit, inverse, scaled = product_norm(0, s, stage_a)
        unit_t[s] = unit
        inv_t[s] = jnp.broadcast_to(inverse, (8, 256))
        mixed = dot(wout_t[0], scaled)
        mixed_s[s] = mixed
        value = held[0, s].astype(jnp.float32) + lin[0, s, 512:640, :] * mixed
        value = value.astype(jnp.bfloat16)
        held[1, s] = value
        input_norm(1, s, value.astype(jnp.float32))
        factor(1, s, 1, stage_b)

    each_slab(middle)
    flush(stage_b, 4)
    each_slab(lambda s: factor(1, s, 0, stage_a))
    flush(stage_a, 3, True)

    def rest_of_middle(s):
        open_gate(1, s)
        gtn[s] = mixed_back(1, s, upper[s].astype(jnp.float32))

    each_slab(rest_of_middle)
    whole(4).wait_recv()
    rows_by_core(3, 4, 5)

    fetch(5, stage_a)

    def turn(s):
        unit, inverse, scaled = product_norm(1, s, stage_a)
        tnorm[s] = scaled
        put(stage_b, s, normalise_back(gtn[s] * gain(1, 1), unit, inverse))

    each_slab(turn)
    flush(stage_b, 6, True)

    def finish(s):
        mixed = dot(wout_t[1], tnorm[s])
        value = held[1, s].astype(jnp.float32) + lin[1, s, 512:640, :] * mixed
        for k in range(2):
            final_ref[2 * s + k] = jnp.transpose(value[:, 128 * k : 128 * k + 128]).astype(
                jnp.bfloat16
            )
        gate_back(1, s, upper[s].astype(jnp.float32), mixed)

    each_slab(finish)
    columns_by_core(3, 6, 8)
    multiply(4, 6, True, 7)
    fetch(8, stage_a)

    def right_back(layer, s):
        gnorm[s] = factor_back(layer, s, 1, stage_a)

    each_slab(lambda s: right_back(1, s))
    fetch(7, stage_b)

    def lower(s):
        value = input_back(1, s, factor_back(1, s, 0, stage_b))
        upper[s] = value
        grad_tnorm = mixed_back(0, s, value.astype(jnp.float32))
        put(stage_a, s, normalise_back(grad_tnorm * gain(0, 1), unit_t[s], inv_t[s, 0:1, :]))

    each_slab(lower)
    flush(stage_a, 9, True)
    each_slab(lambda s: gate_back(0, s, upper[s].astype(jnp.float32), mixed_s[s]))
    rows_by_core(9, 0, 11)
    multiply(9, 1, False, 10)
    fetch(11, stage_a)
    each_slab(lambda s: right_back(0, s))
    fetch(10, stage_b)

    def leave(s):
        value = input_back(0, s, factor_back(0, s, 0, stage_b)).astype(jnp.float32)
        for k in range(2):
            grad_ref[2 * s + k] = jnp.transpose(value[:, 128 * k : 128 * k + 128]).astype(
                jnp.bfloat16
            )

    each_slab(leave)
    for u in range(UNITS):
        whole(u).wait_send()


def local(
    pair_in,
    grad_out,
    token_valid,
    chain_ids,
    chain_table,
    norm_gain,
    norm_offset,
    proj_in,
    proj_out,
):
    vmem = pl.BlockSpec(memory_space=pltpu.VMEM)
    smem = pl.BlockSpec(memory_space=pltpu.SMEM)
    bf16, f32 = jnp.bfloat16, jnp.float32
    scratch = [
        pltpu.VMEM((10, 128, 128), f32),
        pltpu.VMEM((2, 640, 128), bf16),
        pltpu.VMEM((2, 128, 128), bf16),
        pltpu.VMEM((SLABS, 8, 256), f32),
        pltpu.VMEM((2, SLABS, 128, 256), bf16),
        pltpu.VMEM((SLABS, 128, 256), bf16),
        pltpu.VMEM((2, SLABS, 640, 256), f32),
        pltpu.VMEM((SLABS, 128, 256), f32),
        pltpu.VMEM((SLABS, 8, 256), f32),
        pltpu.VMEM((SLABS, 128, 256), f32),
        pltpu.VMEM((SLABS, 128, 256), f32),
        pltpu.VMEM((SLABS, 128, 256), bf16),
        pltpu.VMEM((SLABS, 128, 256), f32),
        pltpu.VMEM((SLABS, 128, 256), bf16),
        pltpu.VMEM((2048, 128), f32),
        pltpu.VMEM((2048, 128), f32),
        pltpu.VMEM((UNITS, DEVICES, 16, 128), bf16),
        pltpu.VMEM((UNITS, DEVICES, 16, 128), bf16),
        pltpu.SemaphoreType.DMA((UNITS,)),
        pltpu.SemaphoreType.DMA((UNITS, 2)),
    ]
    shape = jax.ShapeDtypeStruct(pair_in.shape, bf16)
    return pl.pallas_call(
        kernel,
        out_shape=(shape, shape),
        in_specs=[vmem, vmem, smem, smem] + [vmem] * 7,
        out_specs=(vmem, vmem),
        scratch_shapes=scratch,
        compiler_params=pltpu.CompilerParams(
            collective_id=0, has_side_effects=True, vmem_limit_bytes=56 * 1024 * 1024
        ),
    )(
        pair_in,
        grad_out,
        token_valid,
        chain_ids,
        token_valid.reshape(4, 128),
        chain_ids.reshape(4, 128),
        chain_table,
        norm_gain.reshape(4, 128),
        norm_offset.reshape(4, 128),
        proj_in,
        proj_out,
    )


def solution(mesh):
    in_specs = (P("row", "ch", None), P("row", "ch", None), P(), P(), P(), P(), P(), P(), P())
    out_specs = (P("row", "ch", None), P("row", "ch", None))
    return jax.shard_map(local, mesh=mesh, in_specs=in_specs, out_specs=out_specs, check_vma=False)
```

```python
import jax
import jax.numpy as jnp
from jax import lax
from jax.sharding import PartitionSpec as P
from jax.experimental import pallas as pl
from jax.experimental.pallas import tpu as pltpu

EPS = 1e-05
MESH = pl.DeviceIdType.MESH
DEVICES = 128
UNITS = 12
FAR_FIRST = (2, 3, 1, 0)
SLABS = 8


def far_first(digit):
    return (digit + 2) - lax.div(digit, 2) * (2 * digit - 1)


def dot(first, second, first_dim=1, second_dim=0):
    return lax.dot_general(
        first,
        second,
        (((first_dim,), (second_dim,)), ((), ())),
        preferred_element_type=jnp.float32,
    )


def normalise(values):
    average = jnp.mean(values, axis=0, keepdims=True)
    centred = values - average
    spread = jnp.mean(centred * centred, axis=0, keepdims=True)
    inverse = lax.rsqrt(spread + EPS)
    return centred * inverse, inverse


def normalise_back(scaled_grad, unit, inverse):
    mean_grad = jnp.mean(scaled_grad, axis=0, keepdims=True)
    mean_prod = jnp.mean(scaled_grad * unit, axis=0, keepdims=True)
    return inverse * (scaled_grad - mean_grad - unit * mean_prod)


def twice(block):
    return jnp.concatenate([block, block], axis=1)


def kernel(
    pair_ref,
    gout_ref,
    valid_s,
    chain_s,
    valid_v,
    chain_v,
    table_ref,
    gain_ref,
    offset_ref,
    win_ref,
    wout_ref,
    final_ref,
    grad_ref,
    par,
    win_t,
    wout_t,
    mask,
    held,
    normed,
    lin,
    unit_t,
    inv_t,
    mixed_s,
    gtn,
    tnorm,
    gnorm,
    upper,
    stage_a,
    stage_b,
    snd,
    rcv,
    ssem,
    rsem,
):
    row, col = lax.axis_index("row"), lax.axis_index("ch")
    z, x = lax.div(row, 8), lax.rem(lax.div(row, 2), 4)
    y, core = lax.div(col, 2) * 2 + lax.rem(row, 2), lax.rem(col, 2)
    me = col * 32 + row

    xs = [lax.rem(x + q, 4) * 2 for q in FAR_FIRST]
    ys = [lax.rem(y + q, 4) for q in FAR_FIRST]
    ys = [(lax.rem(value, 2), lax.div(value, 2) * 2) for value in ys]
    spots = [(x_part + low, high) for x_part in xs for low, high in ys]

    def by_core(t):
        plane = lax.rem(z + far_first(lax.rem(t, 4)), 4)
        return plane, lax.rem(core + 1 - lax.div(t, 4), 2), lax.div(t, 4)

    def by_half(t):
        plane = lax.rem(z + far_first(2 * lax.div(t, 4) + lax.rem(t, 2)), 4)
        return plane, lax.rem(core + 1 - lax.rem(lax.div(t, 2), 2), 2), lax.div(t, 4)

    def to_each(act, order, first, count, with_self):
        def step(t, carry):
            plane, core2, part = order(t)
            for r_part, h_part in spots:
                act(plane * 8 + r_part, core2 + h_part, part)
            return carry

        lax.fori_loop(first, first + count - (1 if with_self else 0), step, 0)
        if with_self:
            part = order(jnp.int32(first + count - 1))[2]
            for r_part, h_part in spots[:-1]:
                act(z * 8 + r_part, core + h_part, part)

    barrier = pltpu.get_barrier_semaphore()
    to_each(
        lambda r2, h2, part: pl.semaphore_signal(
            barrier, inc=1, device_id=(r2, h2), device_id_type=MESH
        ),
        by_core,
        0,
        8,
        True,
    )

    def copy_to(u, split):
        def act(r2, h2, part):
            pltpu.make_async_remote_copy(
                src_ref=snd.at[u, h2 * 32 + r2],
                dst_ref=rcv.at[u, me],
                send_sem=ssem.at[u],
                recv_sem=rsem.at[u, part if split else 0],
                device_id=(r2, h2),
                device_id_type=MESH,
            ).start()

        return act

    def keep(u):
        rcv[u, me] = snd[u, me]

    def send(u, split=False, order=by_core):
        keep(u)
        to_each(copy_to(u, split), order, 0, 8, True)

    def whole(u, part=0, count=DEVICES - 1):
        return pltpu.make_async_remote_copy(
            src_ref=snd.at[u, pl.ds(0, count)],
            dst_ref=rcv.at[u, pl.ds(0, count)],
            send_sem=ssem.at[u],
            recv_sem=rsem.at[u, part],
            device_id=(row, col),
            device_id_type=MESH,
        )

    def wait_part(u, part):
        whole(u, part, 64 - part).wait_recv()

    def each_slab(body):
        def step(s, carry):
            body(s)
            return carry

        lax.fori_loop(0, SLABS, step, 0, unroll=8)

    def put(stage, s, value):
        stage[pl.ds(2 * s, 128, stride=16), :] = value[:, :128]
        stage[pl.ds(2 * s + 1, 128, stride=16), :] = value[:, 128:]

    def get(stage, s):
        return jnp.concatenate(
            [stage[pl.ds(2 * s, 128, stride=16), :], stage[pl.ds(2 * s + 1, 128, stride=16), :]],
            axis=1,
        )

    def flush(stage, u, split=False, order=by_core):
        def step(q, carry):
            part = stage[pl.ds(pl.multiple_of(q * 256, 256), 256), :]
            snd[u, pl.ds(q * 16, 16)] = part.astype(jnp.bfloat16).reshape(16, 16, 128)
            return carry

        lax.fori_loop(0, 8, step, 0, unroll=8)
        send(u, split, order)

    def fetch(u, stage):
        whole(u).wait_recv()

        def step(q, carry):
            part = rcv[u, pl.ds(q * 16, 16)].reshape(256, 128)
            stage[pl.ds(pl.multiple_of(q * 256, 256), 256), :] = part.astype(jnp.float32)
            return carry

        lax.fori_loop(0, 8, step, 0, unroll=8)

    def gain(layer, which):
        return twice(par[2 + 2 * layer + which])

    def offset(layer, which):
        return twice(par[6 + 2 * layer + which])

    def column(row_values):
        return jnp.transpose(jnp.broadcast_to(row_values, (128, 128)))

    def prepare(layer):
        for which in range(2):
            k = 2 * layer + which
            par[2 + k] = column(gain_ref[k : k + 1, :])
            par[6 + k] = column(offset_ref[k : k + 1, :])
        for part in range(5):
            block = win_ref[layer, :, part * 128 : (part + 1) * 128].astype(jnp.float32)
            win_t[layer, part * 128 : (part + 1) * 128, :] = jnp.transpose(block).astype(
                jnp.bfloat16
            )
        wout_t[layer] = jnp.transpose(wout_ref[layer].astype(jnp.float32)).astype(jnp.bfloat16)

    def matrix(u, first=0, count=32):
        return jnp.concatenate(
            [
                rcv[u, 32 * h + first : 32 * h + first + count].reshape(16 * count, 128)
                for h in range(4)
            ],
            axis=1,
        )

    def column_of(u, h):
        return rcv[u, pl.ds(32 * h, 32)].reshape(512, 128)

    def plane_rows(u, plane):
        return jnp.concatenate(
            [rcv[u, pl.ds(32 * h + 8 * plane, 8)].reshape(128, 128) for h in range(4)], axis=1
        )

    def store_rows(u, plane, result):
        result = result.astype(jnp.bfloat16)
        for h in range(4):
            part = result[:, 128 * h : 128 * h + 128]
            snd[u, pl.ds(32 * h + 8 * plane, 8)] = part.reshape(8, 16, 128)

    def multiply(u_first, u_second, flip_second, u_out):
        second = matrix(u_second)
        for m in range(2):
            result = dot(matrix(u_first, 16 * m, 16), second, 1, 1 if flip_second else 0)
            result = result.astype(jnp.bfloat16)
            for h in range(4):
                snd[u_out, 32 * h + 16 * m : 32 * h + 16 * m + 16] = result[
                    :, 128 * h : 128 * h + 128
                ].reshape(16, 16, 128)
        send(u_out)

    def rows_by_half(u_first, u_second, u_out):
        second = matrix(u_second)
        for part in range(2):
            wait_part(u_first, part)
            planes = [lax.rem(z + 4 - FAR_FIRST[2 * part + k], 4) for k in range(2)]
            both = jnp.concatenate([plane_rows(u_first, plane) for plane in planes], axis=0)
            result = dot(both, second, 1, 1)
            for k in range(2):
                store_rows(u_out, planes[k], result[128 * k : 128 * k + 128])

            def order(t):
                step = 3 - 3 * lax.rem(t, 2) if part else 2 - lax.rem(t, 2)
                return lax.rem(z + step, 4), lax.rem(core + 1 - lax.div(t, 2), 2), 0

            if part:
                keep(u_out)
            to_each(copy_to(u_out, False), order, 0, 4, part == 1)

    def rows_by_core(u_first, u_second, u_out):
        second = matrix(u_second)
        act = copy_to(u_out, False)
        for part in range(2):
            wait_part(u_first, part)
            own = lax.rem(core + 1 - part, 2)
            planes = [own, own + 2]
            both = jnp.concatenate([column_of(u_first, h) for h in planes], axis=1)
            result = dot(both, second, 0, 0)
            for k in range(2):
                store_rows(u_out, planes[k], result[128 * k : 128 * k + 128])

            def step(t, carry):
                plane = own + 2 * lax.rem(t, 2)
                core2 = lax.rem(core + 1 - lax.div(t, 2), 2)
                for r_part, h_part in spots[:-1]:
                    act(plane * 8 + r_part, core2 + h_part, 0)
                r_part, h_part = spots[-1]

                @pl.when(jnp.logical_or(plane != z, core2 != core))
                def _():
                    act(plane * 8 + r_part, core2 + h_part, 0)

                return carry

            lax.fori_loop(0, 4, step, 0)
        keep(u_out)

    def columns_by_core(u_first, u_second, u_out):
        first = matrix(u_first)
        for part in range(2):
            wait_part(u_second, part)
            own = lax.rem(core + 1 - part, 2)
            columns = [own, own + 2]
            both = jnp.concatenate([column_of(u_second, h) for h in columns], axis=1)
            result = dot(first, both, 1, 0).astype(jnp.bfloat16)
            for k in range(2):
                block = result[:, 128 * k : 128 * k + 128]
                snd[u_out, pl.ds(32 * columns[k], 32)] = block.reshape(32, 16, 128)
            if part:
                keep(u_out)
            to_each(copy_to(u_out, False), by_core, 4 * part, 4, part == 1)

    def factor(layer, s, part, stage):
        both = dot(win_t[layer, 256 * part : 256 * part + 256, :], normed[s])
        squash = jax.nn.sigmoid(both[:128])
        value = both[128:]
        lin[layer, s, 256 * part : 256 * part + 128, :] = squash
        lin[layer, s, 256 * part + 128 : 256 * part + 256, :] = value
        put(stage, s, mask[s, 0:1, :] * (squash * value))

    def input_norm(layer, s, values):
        unit, _ = normalise(values)
        normed[s] = (unit * gain(layer, 0) + offset(layer, 0)).astype(jnp.bfloat16)

    def open_gate(layer, s):
        lin[layer, s, 512:640, :] = jax.nn.sigmoid(dot(win_t[layer, 512:640, :], normed[s]))

    def product_norm(layer, s, stage):
        unit, inverse = normalise(get(stage, s))
        return unit, inverse, (unit * gain(layer, 1) + offset(layer, 1)).astype(jnp.bfloat16)

    def mixed_back(layer, s, upstream):
        grad_mixed = (upstream * lin[layer, s, 512:640, :]).astype(jnp.bfloat16)
        return dot(wout_ref[layer], grad_mixed)

    def gate_back(layer, s, upstream, mixed):
        gate = lin[layer, s, 512:640, :]
        back = (upstream * mixed * gate * (1.0 - gate)).astype(jnp.bfloat16)
        gnorm[s] = dot(win_ref[layer, :, 512:640], back)

    def factor_back(layer, s, part, stage):
        squash = lin[layer, s, 256 * part : 256 * part + 128, :]
        value = lin[layer, s, 256 * part + 128 : 256 * part + 256, :]
        cotangent = mask[s, 0:1, :] * get(stage, s)
        last = cotangent * squash
        first = last * value * (1.0 - squash)
        both = jnp.concatenate([first.astype(jnp.bfloat16), last.astype(jnp.bfloat16)], axis=0)
        return gnorm[s] + dot(win_ref[layer, :, 256 * part : 256 * part + 256], both)

    def input_back(layer, s, grad_normed):
        unit, inverse = normalise(held[layer, s].astype(jnp.float32))
        back = normalise_back(grad_normed * gain(layer, 0), unit, inverse)
        return (upper[s].astype(jnp.float32) + back).astype(jnp.bfloat16)

    par[0] = column(table_ref[0:1, :])
    par[1] = column(table_ref[1:2, :])
    prepare(0)
    valid_cols = valid_v[pl.ds(col, 1), :].astype(jnp.float32)
    chain_cols = chain_v[pl.ds(col, 1), :]

    def enter(s):
        parts, masks = [], []
        for k in range(2):
            at = row * 16 + 2 * s + k
            masks.append(valid_s[at].astype(jnp.float32) * valid_cols)
            same = (chain_cols == chain_s[at]).astype(jnp.float32)
            block = jnp.transpose(pair_ref[2 * s + k].astype(jnp.float32))
            parts.append(block + same * par[1] + (1.0 - same) * par[0])
        mask[s] = jnp.broadcast_to(jnp.concatenate(masks, axis=1), (8, 256))
        entry = jnp.concatenate(parts, axis=1).astype(jnp.bfloat16)
        held[0, s] = entry
        input_norm(0, s, entry.astype(jnp.float32))
        factor(0, s, 0, stage_a)

    each_slab(enter)
    pl.semaphore_wait(barrier, DEVICES - 1)
    flush(stage_a, 0)
    each_slab(lambda s: factor(0, s, 1, stage_b))
    flush(stage_b, 1)

    def rest_of_entry(s):
        open_gate(0, s)
        parts = [jnp.transpose(gout_ref[2 * s + k].astype(jnp.float32)) for k in range(2)]
        upper[s] = jnp.concatenate(parts, axis=1).astype(jnp.bfloat16)

    each_slab(rest_of_entry)
    prepare(1)
    whole(0).wait_recv()
    whole(1).wait_recv()
    multiply(0, 1, True, 2)

    fetch(2, stage_a)

    def middle(s):
        unit, inverse, scaled = product_norm(0, s, stage_a)
        unit_t[s] = unit
        inv_t[s] = jnp.broadcast_to(inverse, (8, 256))
        mixed = dot(wout_t[0], scaled)
        mixed_s[s] = mixed
        value = held[0, s].astype(jnp.float32) + lin[0, s, 512:640, :] * mixed
        value = value.astype(jnp.bfloat16)
        held[1, s] = value
        input_norm(1, s, value.astype(jnp.float32))
        factor(1, s, 1, stage_b)

    each_slab(middle)
    flush(stage_b, 4)
    each_slab(lambda s: factor(1, s, 0, stage_a))
    flush(stage_a, 3, True)

    def rest_of_middle(s):
        open_gate(1, s)
        gtn[s] = mixed_back(1, s, upper[s].astype(jnp.float32))

    each_slab(rest_of_middle)
    whole(4).wait_recv()
    rows_by_core(3, 4, 5)

    fetch(5, stage_a)

    def turn(s):
        unit, inverse, scaled = product_norm(1, s, stage_a)
        tnorm[s] = scaled
        put(stage_b, s, normalise_back(gtn[s] * gain(1, 1), unit, inverse))

    each_slab(turn)
    flush(stage_b, 6, True)

    def finish(s):
        mixed = dot(wout_t[1], tnorm[s])
        value = held[1, s].astype(jnp.float32) + lin[1, s, 512:640, :] * mixed
        for k in range(2):
            final_ref[2 * s + k] = jnp.transpose(value[:, 128 * k : 128 * k + 128]).astype(
                jnp.bfloat16
            )
        gate_back(1, s, upper[s].astype(jnp.float32), mixed)

    each_slab(finish)
    columns_by_core(3, 6, 8)
    multiply(4, 6, True, 7)
    fetch(8, stage_a)

    def right_back(layer, s):
        gnorm[s] = factor_back(layer, s, 1, stage_a)

    each_slab(lambda s: right_back(1, s))
    fetch(7, stage_b)

    def lower(s):
        value = input_back(1, s, factor_back(1, s, 0, stage_b))
        upper[s] = value
        grad_tnorm = mixed_back(0, s, value.astype(jnp.float32))
        put(stage_a, s, normalise_back(grad_tnorm * gain(0, 1), unit_t[s], inv_t[s, 0:1, :]))

    each_slab(lower)
    flush(stage_a, 9, True)
    each_slab(lambda s: gate_back(0, s, upper[s].astype(jnp.float32), mixed_s[s]))
    rows_by_core(9, 0, 11)
    multiply(9, 1, False, 10)
    fetch(11, stage_a)
    each_slab(lambda s: right_back(0, s))
    fetch(10, stage_b)

    def leave(s):
        value = input_back(0, s, factor_back(0, s, 0, stage_b)).astype(jnp.float32)
        for k in range(2):
            grad_ref[2 * s + k] = jnp.transpose(value[:, 128 * k : 128 * k + 128]).astype(
                jnp.bfloat16
            )

    each_slab(leave)
    for u in range(UNITS):
        whole(u).wait_send()


def hand_over(first_in, second_in, first_out, second_out):
    first_out[...] = first_in[...]
    second_out[...] = second_in[...]


def local(
    pair_in,
    grad_out,
    token_valid,
    chain_ids,
    chain_table,
    norm_gain,
    norm_offset,
    proj_in,
    proj_out,
):
    vmem = pl.BlockSpec(memory_space=pltpu.VMEM)
    smem = pl.BlockSpec(memory_space=pltpu.SMEM)
    bf16, f32 = jnp.bfloat16, jnp.float32
    scratch = [
        pltpu.VMEM((10, 128, 128), f32),
        pltpu.VMEM((2, 640, 128), bf16),
        pltpu.VMEM((2, 128, 128), bf16),
        pltpu.VMEM((SLABS, 8, 256), f32),
        pltpu.VMEM((2, SLABS, 128, 256), bf16),
        pltpu.VMEM((SLABS, 128, 256), bf16),
        pltpu.VMEM((2, SLABS, 640, 256), f32),
        pltpu.VMEM((SLABS, 128, 256), f32),
        pltpu.VMEM((SLABS, 8, 256), f32),
        pltpu.VMEM((SLABS, 128, 256), f32),
        pltpu.VMEM((SLABS, 128, 256), f32),
        pltpu.VMEM((SLABS, 128, 256), bf16),
        pltpu.VMEM((SLABS, 128, 256), f32),
        pltpu.VMEM((SLABS, 128, 256), bf16),
        pltpu.VMEM((2048, 128), f32),
        pltpu.VMEM((2048, 128), f32),
        pltpu.VMEM((UNITS, DEVICES, 16, 128), bf16),
        pltpu.VMEM((UNITS, DEVICES, 16, 128), bf16),
        pltpu.SemaphoreType.DMA((UNITS,)),
        pltpu.SemaphoreType.DMA((UNITS, 2)),
    ]
    shape = jax.ShapeDtypeStruct(pair_in.shape, bf16)
    outs = pl.pallas_call(
        kernel,
        out_shape=(shape, shape),
        in_specs=[vmem, vmem, smem, smem] + [vmem] * 7,
        out_specs=(vmem, vmem),
        scratch_shapes=scratch,
        compiler_params=pltpu.CompilerParams(
            collective_id=0, has_side_effects=True, vmem_limit_bytes=56 * 1024 * 1024
        ),
    )(
        pair_in,
        grad_out,
        token_valid,
        chain_ids,
        token_valid.reshape(4, 128),
        chain_ids.reshape(4, 128),
        chain_table,
        norm_gain.reshape(4, 128),
        norm_offset.reshape(4, 128),
        proj_in,
        proj_out,
    )
    rows = pl.BlockSpec((8, 128, 128), lambda i: (i, 0, 0))
    return pl.pallas_call(
        hand_over,
        out_shape=(shape, shape),
        grid=(2,),
        in_specs=[rows, rows],
        out_specs=(rows, rows),
    )(*outs)


def solution(mesh):
    in_specs = (P("row", "ch", None), P("row", "ch", None), P(), P(), P(), P(), P(), P(), P())
    out_specs = (P("row", "ch", None), P("row", "ch", None))
    return jax.shard_map(local, mesh=mesh, in_specs=in_specs, out_specs=out_specs, check_vma=False)
```
